256 devices in a mesh: dp: 16 (over x, y), mp: 16 (over z, core).
Axes of the slice: x: 4, y: 4, z: 8, core: 2. Of those that a mesh axis runs over, the one named last changes fastest.
Arguments:
- patches: bfloat16 [8192, 6144], P('dp', 'mp'), may hold values from -1100 to 1100
- image_counts: int32 [256], P('dp'), may hold values from 8 to 32, as said below
- image_seq: int32 [256], P('dp'), may hold values from 0 to 63, as said below
- image_offset: int32 [256], P('dp'), may hold values from 0 to 96, as said below
- segment_ids: int32 [64, 128], P('dp'), may hold values from -1 to 3, as said below
- norm_gain: bfloat16 [6144], P('mp'), may hold values from 0.099609375 to 1.8984375
- w_up: bfloat16 [6144, 12288], P('dp', 'mp'), may hold values from -2 to 2
- grad_hidden: bfloat16 [8192, 12288], P('dp', 'mp'), may hold values from -150 to 150
Outputs:
- gelu_out: bfloat16 [8192, 12288], P('dp', 'mp')
- grad_w_up: float32 [6144, 12288], P('dp', 'mp')
- grad_gain: float32 [6144], P('mp')
- grad_packed: bfloat16 [8192, 6144], P('dp', 'mp')
The draws below stay inside these ranges and needn't reach their ends.
Inputs may be any that keep to these rules, and one draw needn't show every extreme that they name: `image_counts`: the images of one loader lie back to back from its first row in the given order; loader rows after them are not used. `image_seq`: index d of dp holds sequences d * 4 to (d + 1) * 4 - 1. Every sequence holds exactly 4 images, and every loader sends exactly 1 images to every index of dp, so at most 32 patch rows go from one loader to one index of dp. In every draw some index of dp receives images of 32 rows only, so 32 rows from every loader and 512 filled rows. `image_offset`: the images of one sequence lie back to back from offset 0 without intersection. `segment_ids`: row p of sequence s holds the number, counted from 0 in order of offset, of the image of that sequence that covers it, or -1 where no image does; -1 stands only after the last image.
All inputs are finite; a program needn't handle non-finite values.
Results may differ from the reference program's by a relative error of at most 0.03.
Values may be sent and summed in bfloat16 or wider, within the bound.
No kernel may reach another device: no remote copies, remote signals or barrier semaphores. Data moves between devices by JAX's collectives and lax.ppermute only.
A program may use at most 128 MiB of HBM per device.

```python
import math
import jax
import jax.numpy as jnp
from jax import lax

D = 6144
FFW = 12288
SEQ_LEN = 128
IMG_SEQ = 4
IMG_MIN = 8
SEQ_DEV = 4
IMG_MAX = 32
TOK_DEV = 512
IMG_DEV = 16
SEQS = 64
TOKENS = 8192
IMAGES = 256
N_DP = 16
N_MP = 16


def packing(key):
    key_size, key_full, key_perm, key_tie = jax.random.split(key, 4)
    image_sizes = jax.random.randint(key_size, (N_DP, IMG_DEV), IMG_MIN, IMG_MAX + 1)
    full_dest = jax.random.randint(key_full, (), 0, N_DP)
    dest_ids = jnp.arange(N_DP, dtype=jnp.int32)
    image_sizes = jnp.where(dest_ids[:, None] == full_dest, IMG_MAX, image_sizes).astype(jnp.int32)
    slot_ids = jnp.arange(IMG_DEV, dtype=jnp.int32)
    scores = jax.random.randint(key_perm, (N_DP, IMG_DEV), 0, 1 << 20) * IMG_DEV + slot_ids[None, :]
    shuffled = jnp.argsort(scores, axis=1).astype(jnp.int32)
    source = (shuffled + dest_ids[:, None]) % N_DP
    sequence = dest_ids[:, None] * SEQ_DEV + slot_ids[None, :] // IMG_SEQ
    per_seq = image_sizes.reshape(SEQS, IMG_SEQ)
    seq_ends = jnp.cumsum(per_seq, axis=1).astype(jnp.int32)
    offsets = (seq_ends - per_seq).reshape(N_DP, IMG_DEV)
    tie_ranks = jax.random.permutation(key_tie, IMAGES).astype(jnp.int32)
    loader_order = jnp.argsort(source.reshape(-1) * IMAGES + tie_ranks).astype(jnp.int32)
    positions = jnp.arange(SEQ_LEN, dtype=jnp.int32)
    covered = jnp.sum((positions[None, :, None] >= seq_ends[:, None, :]).astype(jnp.int32), axis=2)
    segments = jnp.where(covered >= IMG_SEQ, -1, covered).astype(jnp.int32)
    counts_out = image_sizes.reshape(-1)[loader_order].astype(jnp.int32)
    seq_out = sequence.reshape(-1)[loader_order].astype(jnp.int32)
    offset_out = offsets.reshape(-1)[loader_order].astype(jnp.int32)
    return (counts_out, seq_out, offset_out, segments)


def packed_source(counts, seqs, offsets):
    loader_counts = counts.reshape(N_DP, IMG_DEV)
    image_ends = jnp.cumsum(loader_counts, axis=1).astype(jnp.int32)
    loader_base = (jnp.arange(N_DP, dtype=jnp.int32) * TOK_DEV)[:, None]
    first_row = (image_ends - loader_counts + loader_base).reshape(-1).astype(jnp.int32)
    patch_step = jnp.arange(IMG_MAX, dtype=jnp.int32)
    inside = patch_step[None, :] < counts[:, None]
    target_row = jnp.where(inside, seqs[:, None] * SEQ_LEN + offsets[:, None] + patch_step[None, :], TOKENS)
    target_row = target_row.reshape(-1).astype(jnp.int32)
    source_row = jnp.minimum(first_row[:, None] + patch_step[None, :], TOKENS - 1).reshape(-1).astype(jnp.int32)
    source_of = jnp.zeros((TOKENS + 1,), jnp.int32).at[target_row].set(source_row)[:TOKENS]
    filled = jnp.zeros((TOKENS + 1,), jnp.int32).at[target_row].set(1)[:TOKENS]
    return (source_of, filled)


def patch_parts(key):
    key_base, key_row, key_col = jax.random.split(key, 3)
    column = jnp.arange(D, dtype=jnp.float32) / D
    col_scale = jnp.exp(jax.random.uniform(key_col, (1, D), minval=0.0, maxval=math.log(10.0)))
    base_values = jnp.clip(jax.random.normal(key_base, (TOKENS, D)), -6.0, 6.0)
    rising = jnp.exp(0.5 * math.log(3.0) * column)
    row_scale = jnp.exp(jax.random.uniform(key_row, (TOKENS, 1), minval=0.0, maxval=math.log(10.0)))
    return (base_values, row_scale * col_scale * rising[None, :])


def draw_image_counts(key, part):
    shared = packing(key)
    return shared[0]


def draw_image_seq(key, part):
    shared = packing(key)
    return shared[1]


def draw_image_offset(key, part):
    shared = packing(key)
    return shared[2]


def draw_segment_ids(key, part):
    shared = packing(key)
    return shared[3]


def draw_patches(key, part):
    key = jax.random.fold_in(key, 11)
    base_values, factor = patch_parts(key)
    return (base_values * factor).astype(jnp.bfloat16)


def draw_grad_hidden(key, part):
    base_values, factor = patch_parts(jax.random.fold_in(key, 11))
    counts, seqs, offsets, segments = packing(key)
    source_of, filled = packed_source(counts, seqs, offsets)
    key = jax.random.fold_in(key, 12)
    key_base, key_row, key_sign = jax.random.split(key, 3)
    base_packed = jnp.where(filled[:, None] > 0, base_values[source_of], 0.0)
    column_of = jnp.arange(FFW, dtype=jnp.int32) % D
    structure = base_packed[:, column_of]
    row_sign = (2 * jax.random.randint(key_sign, (TOKENS, 1), 0, 2) - 1).astype(jnp.float32)
    row_place = jnp.arange(TOKENS, dtype=jnp.float32)[:, None] / TOKENS
    row_scale = jnp.exp(jax.random.uniform(key_row, (TOKENS, 1), minval=0.0, maxval=math.log(4.0)))
    noise_values = jnp.clip(jax.random.normal(key_base, (TOKENS, FFW)), -6.0, 6.0)
    rising = jnp.exp(math.log(3.0) * row_place)
    return ((noise_values + row_sign * structure) * row_scale * rising).astype(jnp.bfloat16)


def draw_w_up(key, part):
    key = jax.random.fold_in(key, 13)
    key_noise, key_offset = jax.random.split(key, 2)
    noise_values = jnp.clip(jax.random.normal(key_noise, (D, FFW)), -6.0, 6.0)
    offset_values = jnp.clip(jax.random.normal(key_offset, (1, FFW)), -4.0, 4.0)
    paired = (jnp.arange(FFW, dtype=jnp.int32)[None, :] % D == jnp.arange(D, dtype=jnp.int32)[:, None]).astype(jnp.float32)
    return ((noise_values + offset_values) * (1.0 / math.sqrt(D)) + 0.7 * paired).astype(jnp.bfloat16)


def setup_inputs(seed: int = 0) -> dict:
    streams_of = jax.random.split(jax.random.key(seed), 9)
    patches = draw_patches(jax.random.fold_in(streams_of[8], 71), 0)
    image_counts = draw_image_counts(jax.random.fold_in(streams_of[8], 71), 0)
    image_seq = draw_image_seq(jax.random.fold_in(streams_of[8], 71), 0)
    image_offset = draw_image_offset(jax.random.fold_in(streams_of[8], 71), 0)
    segment_ids = draw_segment_ids(jax.random.fold_in(streams_of[8], 71), 0)
    norm_gain = jnp.clip(1.0 + 0.18 * jax.random.normal(streams_of[5], (D,), jnp.float32), 0.099609375, 1.8984375).astype(jnp.bfloat16)
    w_up = draw_w_up(jax.random.fold_in(streams_of[8], 71), 0)
    grad_hidden = draw_grad_hidden(jax.random.fold_in(streams_of[8], 71), 0)
    return {"patches": patches, "image_counts": image_counts, "image_seq": image_seq, "image_offset": image_offset, "segment_ids": segment_ids, "norm_gain": norm_gain, "w_up": w_up, "grad_hidden": grad_hidden}


EPSILON = 1e-06
INV_ROOT2 = 0.7071067811865476
INV_ROOT_TWO_PI = 0.3989422804014327

def reference(patches, image_counts, image_seq, image_offset, segment_ids, norm_gain, w_up, grad_hidden):
    loader_counts = image_counts.reshape(N_DP, IMG_DEV)
    image_ends = jnp.cumsum(loader_counts, axis=1).astype(jnp.int32)
    loader_base = (jnp.arange(N_DP, dtype=jnp.int32) * TOK_DEV)[:, None]
    first_row = (image_ends - loader_counts + loader_base).reshape(-1).astype(jnp.int32)
    patch_step = jnp.arange(IMG_MAX, dtype=jnp.int32)
    inside = patch_step[None, :] < image_counts[:, None]
    target_row = jnp.where(inside, image_seq[:, None] * SEQ_LEN + image_offset[:, None] + patch_step[None, :], TOKENS)
    target_row = target_row.reshape(-1).astype(jnp.int32)
    source_row = jnp.minimum(first_row[:, None] + patch_step[None, :], TOKENS - 1).reshape(-1).astype(jnp.int32)
    source_of = jnp.zeros((TOKENS + 1,), jnp.int32).at[target_row].set(source_row)[:TOKENS]
    filled = jnp.zeros((TOKENS + 1,), jnp.int32).at[target_row].set(1)[:TOKENS]
    packed = jnp.where(filled[:, None] > 0, patches[source_of], jnp.zeros_like(patches[:1]))
    widened = packed.astype(jnp.float32)
    row_mean = lax.optimization_barrier(jnp.sum(widened, axis=1)) / D
    row_var = lax.optimization_barrier(jnp.sum(widened * widened, axis=1)) / D - row_mean * row_mean
    inverse_std = lax.rsqrt(row_var + EPSILON)
    scaled_rows = (widened - row_mean[:, None]) * inverse_std[:, None]
    gain_wide = norm_gain.astype(jnp.float32)
    normed = (scaled_rows * gain_wide[None, :]).astype(jnp.bfloat16)
    hidden_in = jnp.dot(normed, w_up, preferred_element_type=jnp.float32)
    normal_cdf = 0.5 * (1.0 + lax.erf(hidden_in * INV_ROOT2))
    gelu_out = (hidden_in * normal_cdf).astype(jnp.bfloat16)
    gelu_slope = normal_cdf + hidden_in * jnp.exp(-0.5 * hidden_in * hidden_in) * INV_ROOT_TWO_PI
    live_rows = (segment_ids.reshape(-1) >= 0).astype(jnp.float32)
    grad_in = (grad_hidden.astype(jnp.float32) * gelu_slope * live_rows[:, None]).astype(jnp.bfloat16)

    def add_group(running, pair):
        normed_group, grad_group = pair
        term = jnp.dot(normed_group.T, grad_group, preferred_element_type=jnp.float32)
        return (running + lax.optimization_barrier(term.astype(jnp.bfloat16)).astype(jnp.float32), None)
    weight_sum, unused = lax.scan(add_group, jnp.zeros((D, FFW), jnp.float32), (normed.reshape(N_DP, TOK_DEV, D), grad_in.reshape(N_DP, TOK_DEV, FFW)))
    shard_cols = FFW // N_MP

    def add_shard(running, pair):
        weight_block, grad_block = pair
        term = jnp.dot(grad_block, weight_block.T, preferred_element_type=jnp.float32)
        return (running + lax.optimization_barrier(term.astype(jnp.bfloat16)).astype(jnp.float32), None)
    weight_blocks = w_up.reshape(D, N_MP, shard_cols).transpose(1, 0, 2)
    grad_blocks = grad_in.reshape(TOKENS, N_MP, shard_cols).transpose(1, 0, 2)
    grad_normed, unused = lax.scan(add_shard, jnp.zeros((TOKENS, D), jnp.float32), (weight_blocks, grad_blocks))
    grad_scaled = grad_normed * gain_wide[None, :]
    first_mean = lax.optimization_barrier(jnp.sum(grad_scaled, axis=1)) / D
    second_mean = lax.optimization_barrier(jnp.sum(grad_scaled * scaled_rows, axis=1)) / D
    grad_packed = (inverse_std[:, None] * (grad_scaled - first_mean[:, None] - scaled_rows * second_mean[:, None])).astype(jnp.bfloat16)
    grad_scale = 1.0 / math.sqrt(TOKENS)
    grad_gain = lax.optimization_barrier(jnp.sum(grad_normed * scaled_rows, axis=0)) * grad_scale
    grad_w_up = weight_sum * grad_scale
    return (gelu_out, grad_w_up, grad_gain, grad_packed)
```

```python
import math

import jax
import jax.numpy as jnp
from jax import lax
from jax.experimental import pallas as pl
from jax.experimental.pallas import tpu as pltpu
from jax.sharding import PartitionSpec as P

SEQ_LEN = 128
SEQ_DEV = 4
IMG_MAX = 32
SLOT = 48

EPSILON = 1e-06
INV_ROOT2 = 0.7071067811865476
INV_ROOT_TWO_PI = 0.3989422804014327
BF16 = jnp.bfloat16
F32 = jnp.float32
VMEM = pl.BlockSpec(memory_space=pltpu.VMEM)
SMEM = pl.BlockSpec(memory_space=pltpu.SMEM)
ROOM = pltpu.CompilerParams(vmem_limit_bytes=48 * 1024 * 1024)


def dot(a, b, ca, cb):
    return lax.dot_general(a, b, (((ca,), (cb,)), ((), ())), preferred_element_type=F32)


def route_kernel(counts, seqs, offsets, patches, out, pick):
    n_img = counts.shape[0]
    tok = patches.shape[0]
    rows = lax.broadcasted_iota(jnp.int32, (SLOT, tok), 0)
    cols = lax.broadcasted_iota(jnp.int32, (SLOT, tok), 1)
    start = jnp.int32(0)
    for i in range(n_img):
        at = pl.multiple_of(seqs[i] // SEQ_DEV * SLOT, SLOT)
        hit = (cols == rows + start) & (rows < counts[i])
        pick[pl.ds(at, SLOT), :] = jnp.where(hit, 1.0, 0.0).astype(BF16)
        start = start + counts[i]
    out[...] = dot(pick[...], patches[...], 1, 0).astype(BF16)
    tail = SLOT - IMG_MAX
    line = lax.broadcasted_iota(jnp.int32, (tail, patches.shape[1]), 0)
    for i in range(n_img):
        at = pl.multiple_of(seqs[i] // SEQ_DEV * SLOT + IMG_MAX, 16)
        place = seqs[i] % SEQ_DEV * SEQ_LEN + offsets[i]
        mark = jnp.where(line == 0, place // 256, jnp.where(line == 1, place % 256, counts[i]))
        out[pl.ds(at, tail), :] = mark.astype(F32).astype(BF16)


def place_kernel(got, gain, out, pick):
    n = got.shape[0] // SLOT
    tok = pick.shape[1]
    rows = lax.broadcasted_iota(jnp.int32, (SLOT, tok), 0).astype(F32)
    ahead = lax.broadcasted_iota(jnp.int32, (SLOT, tok), 1).astype(F32) - rows
    for i in range(n):
        mark = got[i * SLOT + IMG_MAX : (i + 1) * SLOT, 0:128].astype(F32)
        place = jnp.concatenate([mark[0:1] * 256.0 + mark[1:2]] * (tok // 128), axis=1)
        count = jnp.concatenate([mark[2:3]] * (tok // 128), axis=1)
        hit = (ahead == place) & (rows < count)
        pick[i * SLOT : (i + 1) * SLOT, :] = jnp.where(hit, 1.0, 0.0).astype(BF16)
    out[0:tok, :] = dot(pick[...], got[...], 0, 0).astype(BF16)
    out[tok : tok + 16, :] = jnp.broadcast_to(gain[...].astype(F32), (16, gain.shape[1])).astype(BF16)


def norm_kernel(order, *refs):
    blocks, (normed, gain_all, mean_out, inv_out) = refs[:-4], refs[-4:]
    tok, width = mean_out.shape[0], blocks[0].shape[1]
    full = width * len(blocks)
    step = 32
    for i, block in enumerate(blocks):
        at = pl.multiple_of(order[i] * width, width)
        gain_all[:, pl.ds(at, width)] = block[tok : tok + 16, :]

    def body(r, carry):
        here = pl.ds(pl.multiple_of(r * step, step), step)
        total = jnp.zeros((step, 128), F32)
        squares = jnp.zeros((step, 128), F32)
        for block in blocks:
            for k in range(0, width, 128):
                x = block[here, k : k + 128].astype(F32)
                total += x
                squares += x * x
        mean = jnp.sum(total, axis=1, keepdims=True) / full
        var = jnp.sum(squares, axis=1, keepdims=True) / full - mean * mean
        inv = lax.rsqrt(var + EPSILON)
        mean_out[here, :] = jnp.broadcast_to(mean, (step, 128))
        inv_out[here, :] = jnp.broadcast_to(inv, (step, 128))
        for i, block in enumerate(blocks):
            at = pl.multiple_of(order[i] * width, width)
            gain = block[tok : tok + 16, :].astype(F32)[0:1]
            x = (block[here, :].astype(F32) - mean) * inv * gain
            normed[here, pl.ds(at, width)] = x.astype(BF16)
        return carry

    lax.fori_loop(0, tok // step, body, 0)


def back_kernel(order, core, grad_in, w_rows, out):
    width = out.shape[3]
    term = dot(grad_in[...], w_rows[...], 1, 1).astype(BF16)
    out[0, core[0]] = term[:, :width]
    out[0, 1 - core[0]] = term[:, width:]


def back(order, core, grad_in, weight, width):
    tok, cols = grad_in.shape
    n = order.shape[0]
    return pl.pallas_call(
        back_kernel,
        grid_spec=pltpu.PrefetchScalarGridSpec(
            num_scalar_prefetch=2,
            grid=(n,),
            in_specs=[
                pl.BlockSpec((tok, cols), lambda i, order, core: (0, 0)),
                pl.BlockSpec((2 * width, cols), lambda i, order, core: (order[i], 0)),
            ],
            out_specs=pl.BlockSpec((1, 2, tok, width), lambda i, order, core: (i, 0, 0, 0)),
        ),
        out_shape=jax.ShapeDtypeStruct((n, 2, tok, width), BF16),
        compiler_params=ROOM,
        cost_estimate=pl.CostEstimate(
            flops=4 * n * tok * width * cols, bytes_accessed=8 * n * width * cols, transcendentals=0
        ),
    )(order, core, grad_in, weight)


def on_device(
    patches, image_counts, image_seq, image_offset, segment_ids, norm_gain, w_up, grad_hidden
):
    tok, width = patches.shape
    n_dp, n_mp = lax.axis_size("dp"), lax.axis_size("mp")
    full = width * n_mp
    chips = n_mp // 2
    me = lax.axis_index("mp")
    chip, core = me // 2, me % 2
    sign = 2 * core - 1
    onward = [(i, (i // 2 + 1 - 2 * (i % 2)) % chips * 2 + i % 2) for i in range(n_mp)]
    backward = [(j, i) for i, j in onward]
    across = [(i, i ^ 1) for i in range(n_mp)]

    def move(x, path):
        return lax.ppermute(x, "mp", path)

    weight = lax.all_gather(w_up, "dp", axis=0, tiled=True)

    sent = pl.pallas_call(
        route_kernel,
        in_specs=[SMEM, SMEM, SMEM, VMEM],
        out_specs=VMEM,
        out_shape=jax.ShapeDtypeStruct((n_dp * SLOT, width), BF16),
        scratch_shapes=[pltpu.VMEM((n_dp * SLOT, tok), BF16)],
        compiler_params=ROOM,
    )(image_counts, image_seq, image_offset, patches)
    got = lax.all_to_all(sent, "dp", split_axis=0, concat_axis=0, tiled=True)
    mine = pl.pallas_call(
        place_kernel,
        in_specs=[VMEM, VMEM],
        out_specs=VMEM,
        out_shape=jax.ShapeDtypeStruct((tok + 16, width), BF16),
        scratch_shapes=[pltpu.VMEM((n_dp * SLOT, tok), BF16)],
        compiler_params=ROOM,
    )(got, norm_gain.reshape(1, width))

    other = move(mine, across)
    blocks = [mine, other]
    order = [2 * chip + core, 2 * chip + 1 - core]
    near, far = mine, other
    passed = []
    for s in range(1, chips // 2 + 1):
        near = move(near, onward)
        passed.append((near, s, 0))
        if s < chips // 2:
            far = move(far, onward)
            passed.append((far, s, 1))
    for block, s, flip in passed:
        blocks.append(block)
        order.append((chip + sign * s) % chips * 2 + (core + flip) % 2)
    for block, s, flip in passed:
        blocks.append(move(block, across))
        order.append((chip - sign * s) % chips * 2 + (core + 1 + flip) % 2)
    order = jnp.stack(order).astype(jnp.int32)

    normed, gain_all, mean, inv = pl.pallas_call(
        norm_kernel,
        in_specs=[SMEM] + [VMEM] * n_mp,
        out_specs=[VMEM] * 4,
        out_shape=[
            jax.ShapeDtypeStruct((tok, full), BF16),
            jax.ShapeDtypeStruct((16, full), BF16),
            jax.ShapeDtypeStruct((tok, 128), F32),
            jax.ShapeDtypeStruct((tok, 128), F32),
        ],
        compiler_params=ROOM,
    )(order, *blocks)
    row_mean, inverse_std = mean[:, 0:1], inv[:, 0:1]
    gain_local = norm_gain.astype(F32)[None, :]

    hidden_in = jnp.dot(normed, weight, preferred_element_type=F32)
    normal_cdf = 0.5 * (1.0 + lax.erf(hidden_in * INV_ROOT2))
    gelu_out = (hidden_in * normal_cdf).astype(BF16)
    slope = normal_cdf + hidden_in * jnp.exp(-0.5 * hidden_in * hidden_in) * INV_ROOT_TWO_PI
    live_rows = (segment_ids.reshape(-1) >= 0).astype(F32)
    grad_in = (grad_hidden.astype(F32) * slope * live_rows[:, None]).astype(BF16)

    gain_hidden = jnp.dot(gain_all, weight, preferred_element_type=F32)[0:1]
    wide_in = grad_in.astype(F32)
    first_part = jnp.sum(wide_in * gain_hidden, axis=1)
    second_part = jnp.sum(wide_in * hidden_in, axis=1)
    parts = jnp.concatenate([first_part, second_part])[None, :]
    parts = lax.all_to_all(
        jnp.broadcast_to(parts, (n_mp, 2 * tok)), "mp", split_axis=0, concat_axis=0, tiled=True
    )
    sums = jnp.sum(parts, axis=0) / full
    first_mean, second_mean = sums[:tok, None], sums[tok:, None]

    ring = [chip + chips // 2]
    for s in range(chips // 2 - 1, 0, -1):
        ring += [chip + sign * s, chip - sign * s]
    ring = jnp.stack(ring + [chip]).astype(jnp.int32) % chips
    core_at = core.astype(jnp.int32).reshape(1)
    terms = [back(ring[i : i + 1], core_at, grad_in, weight, width)[0] for i in range(chips)]
    far_term, pairs, own = terms[0], terms[1:-1], terms[-1]

    def add(*xs):
        return sum(x.astype(F32) for x in xs).astype(BF16)

    near = add(far_term[0], move(far_term[1], across))
    far = None
    for k in range(0, len(pairs), 2):
        theirs = move(pairs[k + 1], across)
        near = add(pairs[k][0], theirs[1], move(near, backward))
        if far is None:
            far = add(pairs[k][1], theirs[0])
        else:
            far = add(pairs[k][1], theirs[0], move(far, backward))
    near = move(near, backward)
    far = move(far, backward)
    swapped = move(add(far, own[1]), across)
    grad_normed = near.astype(F32) + own[0].astype(F32) + swapped.astype(F32)

    scaled_rows = (mine[:tok].astype(F32) - row_mean) * inverse_std
    grad_packed = (
        inverse_std * (grad_normed * gain_local - first_mean - scaled_rows * second_mean)
    ).astype(BF16)
    grad_scale = 1.0 / math.sqrt(tok * n_dp)
    gain_part = jnp.sum(grad_normed * scaled_rows, axis=0)[None, :]
    gain_part = lax.all_to_all(
        jnp.broadcast_to(gain_part, (n_dp, width)), "dp", split_axis=0, concat_axis=0, tiled=True
    )
    grad_gain = jnp.sum(gain_part, axis=0) * grad_scale

    half = grad_in.shape[1] // 2
    sums = []
    for k in (0, half):
        term = lax.dot_general(
            normed,
            grad_in[:, k : k + half],
            (((0,), (0,)), ((), ())),
            preferred_element_type=F32,
        ).astype(BF16)
        sums.append(lax.psum_scatter(term, "dp", scatter_dimension=0, tiled=True))
    grad_w = jnp.concatenate(sums, axis=1).astype(F32) * grad_scale
    return (gelu_out, grad_w, grad_gain, grad_packed)


def solution(mesh):
    return jax.shard_map(
        on_device,
        mesh=mesh,
        in_specs=(
            P("dp", "mp"),
            P("dp"),
            P("dp"),
            P("dp"),
            P("dp", None),
            P("mp"),
            P("dp", "mp"),
            P("dp", "mp"),
        ),
        out_specs=(P("dp", "mp"), P("dp", "mp"), P("mp"), P("dp", "mp")),
        check_vma=False,
    )
```

```python
import math

import jax
import jax.numpy as jnp
from jax import lax
from jax.experimental import pallas as pl
from jax.experimental.pallas import tpu as pltpu
from jax.sharding import PartitionSpec as P

SEQ_LEN = 128
SEQ_DEV = 4
IMG_MAX = 32
SLOT = 48

EPSILON = 1e-06
INV_ROOT2 = 0.7071067811865476
INV_ROOT_TWO_PI = 0.3989422804014327
BF16 = jnp.bfloat16
F32 = jnp.float32
VMEM = pl.BlockSpec(memory_space=pltpu.VMEM)
SMEM = pl.BlockSpec(memory_space=pltpu.SMEM)
ANY = pl.BlockSpec(memory_space=pl.ANY)
ROOM = pltpu.CompilerParams(vmem_limit_bytes=12 * 1024 * 1024)
WIDE = pltpu.CompilerParams(vmem_limit_bytes=44 * 1024 * 1024)
SIDE = 4
RING = (0, -1, 1, 2)
STEP = 16


def dot(a, b, ca, cb):
    return lax.dot_general(a, b, (((ca,), (cb,)), ((), ())), preferred_element_type=F32)


def route_kernel(counts, seqs, offsets, patches, out, pick):
    n_img = counts.shape[0]
    tok = patches.shape[0]
    rows = lax.broadcasted_iota(jnp.int32, (SLOT, tok), 0)
    cols = lax.broadcasted_iota(jnp.int32, (SLOT, tok), 1)
    start = jnp.int32(0)
    for i in range(n_img):
        at = pl.multiple_of(seqs[i] // SEQ_DEV * SLOT, SLOT)
        hit = (cols == rows + start) & (rows < counts[i])
        pick[pl.ds(at, SLOT), :] = jnp.where(hit, 1.0, 0.0).astype(BF16)
        start = start + counts[i]
    out[...] = dot(pick[...], patches[...], 1, 0).astype(BF16)
    tail = SLOT - IMG_MAX
    line = lax.broadcasted_iota(jnp.int32, (tail, patches.shape[1]), 0)
    for i in range(n_img):
        at = pl.multiple_of(seqs[i] // SEQ_DEV * SLOT + IMG_MAX, 16)
        place = seqs[i] % SEQ_DEV * SEQ_LEN + offsets[i]
        mark = jnp.where(line == 0, place // 256, jnp.where(line == 1, place % 256, counts[i]))
        out[pl.ds(at, tail), :] = mark.astype(F32).astype(BF16)


def place_kernel(got, gain, out, pick):
    n = got.shape[0] // SLOT
    tok = pick.shape[1]
    rows = lax.broadcasted_iota(jnp.int32, (SLOT, tok), 0).astype(F32)
    ahead = lax.broadcasted_iota(jnp.int32, (SLOT, tok), 1).astype(F32) - rows
    for i in range(n):
        mark = got[i * SLOT + IMG_MAX : (i + 1) * SLOT, 0:128].astype(F32)
        place = jnp.concatenate([mark[0:1] * 256.0 + mark[1:2]] * (tok // 128), axis=1)
        count = jnp.concatenate([mark[2:3]] * (tok // 128), axis=1)
        hit = (ahead == place) & (rows < count)
        pick[i * SLOT : (i + 1) * SLOT, :] = jnp.where(hit, 1.0, 0.0).astype(BF16)
    out[0:tok, :] = dot(pick[...], got[...], 0, 0).astype(BF16)
    out[tok : tok + 16, :] = jnp.broadcast_to(gain[...].astype(F32), (16, gain.shape[1])).astype(BF16)


def main_kernel(order, rows_in, *refs):
    w = refs[0:5], refs[5:10]
    grad_hidden, live = refs[10:12]
    gelu_out, turned, normed_out, dx_out, row_out = refs[12:17]
    a_up, a_down, b_up, b_down = refs[17:21]
    xs, normed, hidden, grad_in, dx, cols, gains, sem_x, sem_out, sem_dx = refs[21:]
    n, rows, width = rows_in.shape
    tok, units = gelu_out.shape
    full = n * width
    half = units // 2
    chunk = tok // 4

    loads = []
    for k in range(5):
        part = pl.ds(k * chunk, chunk if k < 4 else rows - tok)
        loads.append(pltpu.make_async_copy(rows_in.at[:, part, :], xs.at[:, part, :], sem_x.at[k]))
    for k in (4, 0, 1, 2, 3):
        loads[k].start()

    loads[4].wait()
    for p in range(n):
        gain = xs[order[p], tok:, :]
        gains[p] = gain.astype(F32)[0:8]
        normed[tok:, p * width : (p + 1) * width] = gain
    for k in range(4):
        loads[k].wait()

        def sums(r, carry):
            here = pl.ds(pl.multiple_of(k * chunk + r * STEP, STEP), STEP)
            total = [jnp.zeros((STEP, 128), F32)] * 3
            squares = [jnp.zeros((STEP, 128), F32)] * 3
            for i in range(n):
                for c in range(width // 128):
                    x = xs[i, here, c * 128 : (c + 1) * 128].astype(F32)
                    total[c % 3] += x
                    squares[c % 3] += x * x
            cols[0, here, :] = total[0] + total[1] + total[2]
            cols[1, here, :] = squares[0] + squares[1] + squares[2]
            return carry

        lax.fori_loop(0, chunk // STEP, sums, 0)
        here = slice(k * chunk, (k + 1) * chunk)
        mean = jnp.sum(cols[0, here, :], axis=1, keepdims=True) / full
        var = jnp.sum(cols[1, here, :], axis=1, keepdims=True) / full - mean * mean
        cols[0, here, :] = jnp.broadcast_to(mean, (chunk, 128))
        cols[1, here, :] = jnp.broadcast_to(lax.rsqrt(var + EPSILON), (chunk, 128))

        def scale(r, carry):
            here = pl.ds(pl.multiple_of(k * chunk + r * STEP, STEP), STEP)
            mean = jnp.concatenate([cols[0, here, :]] * (width // 128), axis=1)
            inv = jnp.concatenate([cols[1, here, :]] * (width // 128), axis=1)
            for p in range(n):
                gain = jnp.broadcast_to(gains[p, 0:1, :], (STEP, width))
                x = (xs[order[p], here, :].astype(F32) - mean) * inv * gain
                normed[here, p * width : (p + 1) * width] = x.astype(BF16)
            return carry

        lax.fori_loop(0, chunk // STEP, scale, 0)
    save = pltpu.make_async_copy(normed.at[pl.ds(0, tok), :], normed_out, sem_out)
    save.start()

    def features(places, count):
        return jnp.concatenate([normed[0:count, p * width : (p + 1) * width] for p in places], axis=1)

    def weight_rows(s, q, j, count):
        if q < SIDE - 1:
            return w[s][q][j * width : (j + count) * width, :]
        return w[s][q + j // 2][j % 2 * width : (j % 2 + count) * width, :]

    for s in range(2):
        total = None
        for q in range(SIDE):
            places = [q * SIDE + j if s == 0 else j * SIDE + q for j in range(SIDE)]
            for j in (0, 2):
                if q < SIDE - 1:
                    if j:
                        continue
                    term = dot(features(places, rows), w[s][q][...], 1, 0)
                else:
                    term = dot(features(places[j : j + 2], rows), w[s][q + j // 2][...], 1, 0)
                total = term if total is None else total + term
        hidden[:, s * half : (s + 1) * half] = total

    def epilogue(r, carry):
        here = pl.ds(pl.multiple_of(r * STEP, STEP), STEP)
        h = hidden[here, :]
        cdf = 0.5 * (1.0 + lax.erf(h * INV_ROOT2))
        gelu_out[here, :] = (h * cdf).astype(BF16)
        slope = cdf + h * jnp.exp(-0.5 * h * h) * INV_ROOT_TWO_PI
        lives = jnp.concatenate([live[here, :]] * (units // 128), axis=1)
        g = (grad_hidden[here, :].astype(F32) * slope * lives).astype(BF16)
        grad_in[here, :] = g
        g = g.astype(F32)
        gained = g * hidden[tok : tok + 1, :]
        cols[2, here, :] = jnp.broadcast_to(jnp.sum(gained, axis=1, keepdims=True), (STEP, 128))
        cols[3, here, :] = jnp.broadcast_to(jnp.sum(g * h, axis=1, keepdims=True), (STEP, 128))
        return carry

    lax.fori_loop(0, tok // STEP, epilogue, 0)
    turned[...] = grad_in[...].T
    for k in range(4):
        row_out[k] = cols[k].T[0:8]

    saves = []
    for q in range(SIDE):
        for j in (0, 2):
            first = weight_rows(0, q, j, 2)
            second = jnp.concatenate([weight_rows(1, j + e, q, 1) for e in (0, 1)], axis=0)
            term = dot(jnp.concatenate([first, second], axis=1), turned[...], 1, 0).astype(BF16)
            for e in (0, 1):
                p = q * SIDE + j + e
                dx[p] = term[e * width : (e + 1) * width, :]
                saves.append(pltpu.make_async_copy(dx.at[p], dx_out.at[order[p]], sem_dx.at[p]))
                saves[-1].start()

    last = SIDE - 1
    for j in (0, 1):
        a = features([2 * j * SIDE + last, (2 * j + 1) * SIDE + last], tok)
        (a_up, a_down)[j][...] = dot(turned[0:half, :], a, 1, 0).astype(BF16)
        b = features([last * SIDE + 2 * j, last * SIDE + 2 * j + 1], tok)
        (b_up, b_down)[j][...] = dot(turned[half:, :], b, 1, 0).astype(BF16)
    for copy in saves:
        copy.wait()
    save.wait()


def main(order, gathered, wa, wb, grad_hidden, live):
    n, rows, width = gathered.shape
    tok, units = grad_hidden.shape
    half = units // 2
    shape = jax.ShapeDtypeStruct
    return pl.pallas_call(
        main_kernel,
        in_specs=[SMEM, ANY] + [VMEM] * 12,
        out_specs=[VMEM, VMEM, ANY, ANY] + [VMEM] * 5,
        out_shape=[
            shape((tok, units), BF16),
            shape((units, tok), BF16),
            shape((tok, n * width), BF16),
            shape((n, width, tok), BF16),
            shape((4, 8, tok), F32),
        ]
        + [shape((half, 2 * width), BF16)] * 4,
        scratch_shapes=[
            pltpu.VMEM((n, rows, width), BF16),
            pltpu.VMEM((rows, n * width), BF16),
            pltpu.VMEM((rows, units), F32),
            pltpu.VMEM((tok, units), BF16),
            pltpu.VMEM((n, width, tok), BF16),
            pltpu.VMEM((4, tok, 128), F32),
            pltpu.VMEM((n, 8, width), F32),
            pltpu.SemaphoreType.DMA((5,)),
            pltpu.SemaphoreType.DMA,
            pltpu.SemaphoreType.DMA((n,)),
        ],
        compiler_params=WIDE,
        cost_estimate=pl.CostEstimate(
            flops=5 * tok * units * n * width, bytes_accessed=40 * 2**20, transcendentals=0
        ),
    )(order, gathered, *wa, *wb, grad_hidden, live)


def part_kernel(turned, c0, c1, c2, c3, b, a_out, b_out):
    half = b_out.shape[0]
    a = jnp.concatenate([c0[...], c1[...], c2[...], c3[...]], axis=1)
    a_out[...] = dot(turned[0:half, :], a, 1, 0).astype(BF16)
    b_out[...] = dot(turned[half:, :], b[...], 1, 0).astype(BF16)


def part(normed, turned, q, width):
    units, tok = turned.shape
    half = units // 2
    cut = [pl.BlockSpec((tok, width), lambda i, j=j: (0, j * SIDE + q)) for j in range(SIDE)]
    return pl.pallas_call(
        part_kernel,
        grid=(1,),
        in_specs=[pl.BlockSpec((units, tok), lambda i: (0, 0))]
        + cut
        + [pl.BlockSpec((tok, SIDE * width), lambda i: (0, q))],
        out_specs=[pl.BlockSpec((half, SIDE * width), lambda i: (0, 0))] * 2,
        out_shape=[jax.ShapeDtypeStruct((half, SIDE * width), BF16)] * 2,
        compiler_params=ROOM,
        cost_estimate=pl.CostEstimate(
            flops=2 * tok * units * SIDE * width, bytes_accessed=8 * 2**20, transcendentals=0
        ),
    )(turned, normed, normed, normed, normed, normed)


def along_x(s):
    return [(i, (i // SIDE + s) % SIDE * SIDE + i % SIDE) for i in range(SIDE * SIDE)]


def along_y(s):
    return [(i, i // SIDE * SIDE + (i % SIDE + s) % SIDE) for i in range(SIDE * SIDE)]


def move(x, path):
    return lax.ppermute(x, "dp", path)


def add(*xs):
    return sum(x.astype(F32) for x in xs)


def ring_gather(x, along):
    h = x.shape[0] // 2
    below, above = move(x, along(1)), move(x, along(-1))
    return [x, below, above, move(below[:h], along(1)), move(above[h:], along(-1))]


def ring_sum(own, minus, plus, up, down, along, axis):
    h = up.shape[axis]
    cut = lambda x, a, b: lax.slice_in_dim(x, a, b, axis=axis)
    up, down = move(up, along(1)), move(down, along(-1))
    plus = jnp.concatenate([add(cut(plus, 0, h), up).astype(BF16), cut(plus, h, 2 * h)], axis=axis)
    minus = jnp.concatenate([cut(minus, 0, h), add(cut(minus, h, 2 * h), down).astype(BF16)], axis=axis)
    return add(own, move(plus, along(1)), move(minus, along(-1)))


def on_device(
    patches, image_counts, image_seq, image_offset, segment_ids, norm_gain, w_up, grad_hidden
):
    tok, width = patches.shape
    n_dp, n_mp = lax.axis_size("dp"), lax.axis_size("mp")
    full = width * n_mp
    half = w_up.shape[1] // 2
    me = lax.axis_index("dp")
    places = [
        (me // SIDE + RING[j] + SIDE) % SIDE * SIDE + (me % SIDE + RING[q] + SIDE) % SIDE
        for q in range(SIDE)
        for j in range(SIDE)
    ]
    order = jnp.stack(places).astype(jnp.int32)

    sent = pl.pallas_call(
        route_kernel,
        in_specs=[SMEM, SMEM, SMEM, VMEM],
        out_specs=VMEM,
        out_shape=jax.ShapeDtypeStruct((n_dp * SLOT, width), BF16),
        scratch_shapes=[pltpu.VMEM((n_dp * SLOT, tok), BF16)],
        compiler_params=ROOM,
    )(image_counts, image_seq, image_offset, patches)
    got = lax.all_to_all(sent, "dp", split_axis=0, concat_axis=0, tiled=True)
    mine = pl.pallas_call(
        place_kernel,
        in_specs=[VMEM, VMEM],
        out_specs=VMEM,
        out_shape=jax.ShapeDtypeStruct((tok + 16, width), BF16),
        scratch_shapes=[pltpu.VMEM((n_dp * SLOT, tok), BF16)],
        compiler_params=ROOM,
    )(got, norm_gain.reshape(1, width))
    gathered = lax.all_gather(mine, "mp", axis=0)

    wa = ring_gather(jnp.concatenate(ring_gather(w_up[:, :half], along_x), axis=0), along_y)
    wb = ring_gather(jnp.concatenate(ring_gather(w_up[:, half:], along_y), axis=0), along_x)

    live = jnp.broadcast_to((segment_ids.reshape(tok, 1) >= 0).astype(F32), (tok, 128))
    gelu_out, turned, normed, terms, rows, *opposite = main(
        order, gathered, wa, wb, grad_hidden, live
    )
    row_mean, inverse_std = rows[0, 0:1], rows[1, 0:1]

    grad_normed = lax.psum_scatter(terms, "mp", scatter_dimension=0).astype(F32)

    parts = [part(normed, turned, q, width) for q in (1, 2, 0)]
    (a_minus, b_minus), (a_plus, b_plus), (a_own, b_own) = parts
    a = ring_sum(a_own, a_minus, a_plus, *opposite[0:2], along_x, 1)
    b = ring_sum(b_own, b_minus, b_plus, *opposite[2:4], along_y, 1)

    def finish(x, along):
        cut = [x[:, q * width : (q + 1) * width] for q in range(SIDE)]
        sent = [c.astype(BF16) for c in cut[1:]]
        h = half // 2
        return ring_sum(cut[0], sent[0], sent[1], sent[2][:h], sent[2][h:], along, 0)

    grad_scale = 1.0 / math.sqrt(tok * n_dp)
    grad_w = (jnp.concatenate([finish(a, along_y), finish(b, along_x)], axis=0) * grad_scale).T

    sums = lax.all_to_all(
        jnp.broadcast_to(rows[2:4, 0].reshape(1, 2 * tok), (n_mp, 2 * tok)),
        "mp",
        split_axis=0,
        concat_axis=0,
        tiled=True,
    )
    sums = jnp.sum(sums, axis=0, keepdims=True) / full
    first_mean, second_mean = sums[:, :tok], sums[:, tok:]

    scaled = (mine[:tok].T.astype(F32) - row_mean) * inverse_std
    grad_scaled = grad_normed * norm_gain.astype(F32)[:, None]
    grad_packed = inverse_std * (grad_scaled - first_mean - scaled * second_mean)
    gain_part = jnp.sum(grad_normed * scaled, axis=1)[None, :]
    gain_part = lax.all_to_all(
        jnp.broadcast_to(gain_part, (n_dp, width)), "dp", split_axis=0, concat_axis=0, tiled=True
    )
    grad_gain = jnp.sum(gain_part, axis=0) * grad_scale
    return (gelu_out, grad_w, grad_gain, grad_packed.astype(BF16).T)


def solution(mesh):
    return jax.shard_map(
        on_device,
        mesh=mesh,
        in_specs=(
            P("dp", "mp"),
            P("dp"),
            P("dp"),
            P("dp"),
            P("dp", None),
            P("mp"),
            P("dp", "mp"),
            P("dp", "mp"),
        ),
        out_specs=(P("dp", "mp"), P("dp", "mp"), P("mp"), P("dp", "mp")),
        check_vma=False,
    )
```

```python
import math

import jax
import jax.numpy as jnp
from jax import lax
from jax.experimental import pallas as pl
from jax.experimental.pallas import tpu as pltpu
from jax.sharding import PartitionSpec as P

SEQ_LEN = 128
SEQ_DEV = 4
IMG_MAX = 32
SLOT = 48

EPSILON = 1e-06
INV_ROOT2 = 0.7071067811865476
INV_ROOT_TWO_PI = 0.3989422804014327
BF16 = jnp.bfloat16
F32 = jnp.float32
VMEM = pl.BlockSpec(memory_space=pltpu.VMEM)
SMEM = pl.BlockSpec(memory_space=pltpu.SMEM)
HBM = pl.BlockSpec(memory_space=pltpu.HBM)
WIDE = pltpu.CompilerParams(vmem_limit_bytes=53 * 1024 * 1024)
FULL = pltpu.CompilerParams(vmem_limit_bytes=60 * 1024 * 1024)
ROOM = pltpu.CompilerParams(vmem_limit_bytes=12 * 1024 * 1024)
SIDE = 4
RING = (0, -1, 1, 2)
STEP = 16
NORM_FLOPS = 5 * 10**9
JOIN_FLOPS = 45 * 10**9


def dot(a, b, ca, cb):
    return lax.dot_general(a, b, (((ca,), (cb,)), ((), ())), preferred_element_type=F32)


def route_kernel(tables_in, patches_in, out, pick, tables, patches, sem):
    loads = [
        pltpu.make_async_copy(tables_in, tables, sem.at[0]),
        pltpu.make_async_copy(patches_in, patches, sem.at[1]),
    ]
    for load in loads:
        load.start()
    for load in loads:
        load.wait()
    counts, seqs, offsets = [[tables[k, i] for i in range(tables.shape[1])] for k in range(3)]
    n_img = len(counts)
    tok = patches.shape[0]
    rows = lax.broadcasted_iota(jnp.int32, (SLOT, tok), 0)
    cols = lax.broadcasted_iota(jnp.int32, (SLOT, tok), 1)
    start = jnp.int32(0)
    for i in range(n_img):
        at = pl.multiple_of(seqs[i] // SEQ_DEV * SLOT, SLOT)
        hit = (cols == rows + start) & (rows < counts[i])
        pick[pl.ds(at, SLOT), :] = jnp.where(hit, 1.0, 0.0).astype(BF16)
        start = start + counts[i]
    out[...] = dot(pick[...], patches[...], 1, 0).astype(BF16)
    tail = SLOT - IMG_MAX
    line = lax.broadcasted_iota(jnp.int32, (tail, patches.shape[1]), 0)
    for i in range(n_img):
        at = pl.multiple_of(seqs[i] // SEQ_DEV * SLOT + IMG_MAX, 16)
        place = seqs[i] % SEQ_DEV * SEQ_LEN + offsets[i]
        mark = jnp.where(line == 0, place // 256, jnp.where(line == 1, place % 256, counts[i]))
        out[pl.ds(at, tail), :] = mark.astype(F32).astype(BF16)


def place_kernel(got, gain, out, pick):
    n = got.shape[0] // SLOT
    tok = pick.shape[1]
    rows = lax.broadcasted_iota(jnp.int32, (SLOT, tok), 0).astype(F32)
    ahead = lax.broadcasted_iota(jnp.int32, (SLOT, tok), 1).astype(F32) - rows
    for i in range(n):
        mark = got[i * SLOT + IMG_MAX : (i + 1) * SLOT, 0:128].astype(F32)
        place = jnp.concatenate([mark[0:1] * 256.0 + mark[1:2]] * (tok // 128), axis=1)
        count = jnp.concatenate([mark[2:3]] * (tok // 128), axis=1)
        hit = (ahead == place) & (rows < count)
        pick[i * SLOT : (i + 1) * SLOT, :] = jnp.where(hit, 1.0, 0.0).astype(BF16)
    out[0:tok, :] = dot(pick[...], got[...], 0, 0).astype(BF16)
    out[tok : tok + 16, :] = jnp.broadcast_to(gain[...].astype(F32), (16, gain.shape[1])).astype(BF16)


def norm_kernel(order, rows_in, normed_out, row_out, xs, normed, cols, gains, sem_x, sem_out):
    n, rows, width = rows_in.shape
    tok = row_out.shape[2]
    full = n * width
    chunk = tok // 4
    loads = []
    for k in range(5):
        part = pl.ds(k * chunk, chunk if k < 4 else rows - tok)
        loads.append(pltpu.make_async_copy(rows_in.at[:, part, :], xs.at[:, part, :], sem_x.at[k]))
    for k in (4, 0, 1, 2, 3):
        loads[k].start()

    saves = [pltpu.make_async_copy(normed.at[pl.ds(tok, rows - tok), :], normed_out.at[pl.ds(tok, rows - tok), :], sem_out.at[4])]
    loads[4].wait()
    for p in range(n):
        gain = xs[order[p], tok:, :]
        gains[p] = gain.astype(F32)[0:8]
        normed[tok:, p * width : (p + 1) * width] = gain
    saves[0].start()
    for k in range(4):
        loads[k].wait()

        def sums(r, carry):
            here = pl.ds(pl.multiple_of(k * chunk + r * STEP, STEP), STEP)
            total = [jnp.zeros((STEP, 128), F32)] * 3
            squares = [jnp.zeros((STEP, 128), F32)] * 3
            for i in range(n):
                for c in range(width // 128):
                    x = xs[i, here, c * 128 : (c + 1) * 128].astype(F32)
                    total[c % 3] += x
                    squares[c % 3] += x * x
            cols[0, here, :] = total[0] + total[1] + total[2]
            cols[1, here, :] = squares[0] + squares[1] + squares[2]
            return carry

        lax.fori_loop(0, chunk // STEP, sums, 0)
        here = slice(k * chunk, (k + 1) * chunk)
        mean = jnp.sum(cols[0, here, :], axis=1, keepdims=True) / full
        var = jnp.sum(cols[1, here, :], axis=1, keepdims=True) / full - mean * mean
        cols[0, here, :] = jnp.broadcast_to(mean, (chunk, 128))
        cols[1, here, :] = jnp.broadcast_to(lax.rsqrt(var + EPSILON), (chunk, 128))

        def scale(r, carry):
            here = pl.ds(pl.multiple_of(k * chunk + r * STEP, STEP), STEP)
            mean = jnp.concatenate([cols[0, here, :]] * (width // 128), axis=1)
            inv = jnp.concatenate([cols[1, here, :]] * (width // 128), axis=1)
            for p in range(n):
                gain = jnp.broadcast_to(gains[p, 0:1, :], (STEP, width))
                x = (xs[order[p], here, :].astype(F32) - mean) * inv * gain
                normed[here, p * width : (p + 1) * width] = x.astype(BF16)
            return carry

        lax.fori_loop(0, chunk // STEP, scale, 0)
        part = pl.ds(k * chunk, chunk)
        saves.append(pltpu.make_async_copy(normed.at[part, :], normed_out.at[part, :], sem_out.at[k]))
        saves[-1].start()
    for k in range(2):
        row_out[k] = cols[k].T[0:8]
    for save in saves:
        save.wait()


def norm(order, gathered, tok):
    n, rows, width = gathered.shape
    return pl.pallas_call(
        norm_kernel,
        in_specs=[SMEM, HBM],
        out_specs=[HBM, VMEM],
        out_shape=[
            jax.ShapeDtypeStruct((rows, n * width), BF16),
            jax.ShapeDtypeStruct((2, 8, tok), F32),
        ],
        scratch_shapes=[
            pltpu.VMEM((n, rows, width), BF16),
            pltpu.VMEM((rows, n * width), BF16),
            pltpu.VMEM((2, tok, 128), F32),
            pltpu.VMEM((n, 8, width), F32),
            pltpu.SemaphoreType.DMA((5,)),
            pltpu.SemaphoreType.DMA((5,)),
        ],
        compiler_params=WIDE,
        cost_estimate=pl.CostEstimate(
            flops=NORM_FLOPS, bytes_accessed=4 * n * rows * width, transcendentals=0
        ),
    )(order, gathered)


def main_kernel(order, normed_in, *refs):
    pieces = refs[0:16]
    grad_hidden, live = refs[16:18]
    gelu_out, turned, dx_out, row_out = refs[18:22]
    a_up, a_down, b_up, b_down = refs[22:26]
    normed, w, hidden, grad_in, dx, cols, sem_w, sem_n, sem_dx = refs[26:]
    n, width, tok = dx_out.shape
    rows = normed_in.shape[0]
    units = grad_hidden.shape[1]
    half = units // 2
    loads = [pltpu.make_async_copy(piece, w.at[k], sem_w.at[k]) for k, piece in enumerate(pieces)]
    quarter = SIDE * width
    loads_n = []
    for q in range(SIDE):
        part = (slice(None), pl.ds(q * quarter, quarter))
        loads_n.append(pltpu.make_async_copy(normed_in.at[part], normed.at[part], sem_n.at[q]))
    queue = [load for q in range(SIDE) for load in (loads_n[q], loads[2 * q], loads[2 * q + 1])] + loads[8:]
    for load in queue[:6]:
        load.start()
    later = queue[6:]

    def arrived(load):
        load.wait()
        if later:
            later.pop(0).start()

    def features(places, count):
        return jnp.concatenate([normed[0:count, p * width : (p + 1) * width] for p in places], axis=1)

    def weight_rows(s, q, j, count):
        return w[8 * s + 2 * q + j // 2, j % 2 * width : (j % 2 + count) * width, :]

    for s in range(2):
        total = None
        for q in range(SIDE):
            for j in (0, 2):
                if s == 0 and j == 0:
                    arrived(loads_n[q])
                arrived(loads[8 * s + 2 * q + j // 2])
                places = [q * SIDE + j + e if s == 0 else (j + e) * SIDE + q for e in (0, 1)]
                term = dot(features(places, rows), weight_rows(s, q, j, 2), 1, 0)
                total = term if total is None else total + term
        hidden[:, s * half : (s + 1) * half] = total

    def epilogue(r, carry):
        here = pl.ds(pl.multiple_of(r * STEP, STEP), STEP)
        h = hidden[here, :]
        cdf = 0.5 * (1.0 + lax.erf(h * INV_ROOT2))
        gelu_out[here, :] = (h * cdf).astype(BF16)
        slope = cdf + h * jnp.exp(-0.5 * h * h) * INV_ROOT_TWO_PI
        lives = jnp.concatenate([live[here, :]] * (units // 128), axis=1)
        g = (grad_hidden[here, :].astype(F32) * slope * lives).astype(BF16)
        grad_in[here, :] = g
        g = g.astype(F32)
        gained = g * hidden[tok : tok + 1, :]
        cols[0, here, :] = jnp.broadcast_to(jnp.sum(gained, axis=1, keepdims=True), (STEP, 128))
        cols[1, here, :] = jnp.broadcast_to(jnp.sum(g * h, axis=1, keepdims=True), (STEP, 128))
        return carry

    lax.fori_loop(0, tok // STEP, epilogue, 0)
    turned[...] = grad_in[...].T
    for k in range(2):
        row_out[k] = cols[k].T[0:8]

    saves = []
    for q in range(SIDE):
        for j in (0, 2):
            first = weight_rows(0, q, j, 2)
            second = jnp.concatenate([weight_rows(1, j + e, q, 1) for e in (0, 1)], axis=0)
            term = dot(jnp.concatenate([first, second], axis=1), turned[...], 1, 0).astype(BF16)
            for e in (0, 1):
                p = q * SIDE + j + e
                dx[p] = term[e * width : (e + 1) * width, :]
                saves.append(pltpu.make_async_copy(dx.at[p], dx_out.at[order[p]], sem_dx.at[p]))
                saves[-1].start()

    last = SIDE - 1
    for j, (a_out, b_out) in enumerate(((a_up, b_up), (a_down, b_down))):
        a = features([2 * j * SIDE + last, (2 * j + 1) * SIDE + last], tok)
        a_out[...] = dot(turned[0:half, :], a, 1, 0).astype(BF16)
        b = features([last * SIDE + 2 * j, last * SIDE + 2 * j + 1], tok)
        b_out[...] = dot(turned[half:, :], b, 1, 0).astype(BF16)
    for copy in saves:
        copy.wait()


def main(order, normed, wa, wb, grad_hidden, live):
    n, (rows, full) = order.shape[0], normed.shape
    tok, units = grad_hidden.shape
    shape = jax.ShapeDtypeStruct
    return pl.pallas_call(
        main_kernel,
        in_specs=[SMEM] + [HBM] * 17 + [VMEM, VMEM],
        out_specs=[VMEM, VMEM, HBM] + [VMEM] * 5,
        out_shape=[
            shape((tok, units), BF16),
            shape((units, tok), BF16),
            shape((n, full // n, tok), BF16),
            shape((2, 8, tok), F32),
        ]
        + [shape((units // 2, 2 * full // n), BF16)] * 4,
        scratch_shapes=[
            pltpu.VMEM((rows, full), BF16),
            pltpu.VMEM((n, 2 * full // n, units // 2), BF16),
            pltpu.VMEM((rows, units), F32),
            pltpu.VMEM((tok, units), BF16),
            pltpu.VMEM((n, full // n, tok), BF16),
            pltpu.VMEM((2, tok, 128), F32),
            pltpu.SemaphoreType.DMA((n,)),
            pltpu.SemaphoreType.DMA((SIDE,)),
            pltpu.SemaphoreType.DMA((n,)),
        ],
        compiler_params=FULL,
        cost_estimate=pl.CostEstimate(
            flops=4 * tok * units * full, bytes_accessed=40 * 2**20, transcendentals=0
        ),
    )(order, normed, *wa, *wb, grad_hidden, live)


def part_kernel(turned, c0, c1, c2, c3, b, *outs):
    n = len(outs) // 2
    half, size = outs[0].shape
    for k in range(n):
        a = jnp.concatenate([c[...] for c in (c0, c1, c2, c3)[k * SIDE // n : (k + 1) * SIDE // n]], axis=1)
        outs[k][...] = dot(turned[0:half, :], a, 1, 0).astype(BF16)
        right = b[:, k * size : (k + 1) * size]
        outs[n + k][...] = dot(turned[half:, :], right, 1, 0).astype(BF16)


def part(normed, turned, q, width):
    units, tok = turned.shape
    half = units // 2
    n = 1
    cut = [pl.BlockSpec((tok, width), lambda i, j=j: (0, j * SIDE + q)) for j in range(SIDE)]
    out = (half, SIDE // n * width)
    return pl.pallas_call(
        part_kernel,
        grid=(1,),
        in_specs=[pl.BlockSpec((units, tok), lambda i: (0, 0))]
        + cut
        + [pl.BlockSpec((tok, SIDE * width), lambda i: (0, q))],
        out_specs=[pl.BlockSpec(out, lambda i: (0, 0))] * (2 * n),
        out_shape=[jax.ShapeDtypeStruct(out, BF16)] * (2 * n),
        compiler_params=ROOM,
        cost_estimate=pl.CostEstimate(
            flops=2 * tok * units * SIDE * width, bytes_accessed=8 * 2**20, transcendentals=0
        ),
    )(turned, normed, normed, normed, normed, normed)


def along_x(s):
    return [(i, (i // SIDE + s) % SIDE * SIDE + i % SIDE) for i in range(SIDE * SIDE)]


def along_y(s):
    return [(i, i // SIDE * SIDE + (i % SIDE + s) % SIDE) for i in range(SIDE * SIDE)]


def move(x, path):
    return lax.ppermute(x, "dp", path)


def add(*xs):
    return sum(x.astype(F32) for x in xs)


def opposite_halves(ring, along):
    own, below, above = ring
    h = own.shape[0] // 2
    return [move(below[:h], along(1)), move(above[h:], along(-1))]


def join_kernel(*refs):
    at = 0
    for piece in refs[:-1]:
        refs[-1][at : at + piece.shape[0], :] = piece[...]
        at += piece.shape[0]


def join(pieces):
    rows, cols = sum(x.shape[0] for x in pieces), pieces[0].shape[1]
    return pl.pallas_call(
        join_kernel,
        in_specs=[VMEM] * len(pieces),
        out_specs=VMEM,
        out_shape=jax.ShapeDtypeStruct((rows, cols), BF16),
        compiler_params=ROOM,
        cost_estimate=pl.CostEstimate(flops=JOIN_FLOPS, bytes_accessed=4 * rows * cols, transcendentals=0),
    )(*pieces)


def spread(ring, along, other):
    far = opposite_halves(ring, along)
    low, high = join(ring[:2]), join([ring[2]] + far)
    low = [low, move(low, other(1)), move(low, other(-1))]
    high = [high, move(high, other(1)), move(high, other(-1))]
    low.append(move(low[1], other(1)))
    high.append(move(high[2], other(-1)))
    return [x for pair in zip(low, high) for x in pair]


def ring_meet(minus, plus, up, down, along, axis):
    h = up.shape[axis]
    cut = lambda x, a, b: lax.slice_in_dim(x, a, b, axis=axis)
    up, down = move(up, along(1)), move(down, along(-1))
    plus = jnp.concatenate([add(cut(plus, 0, h), up).astype(BF16), cut(plus, h, 2 * h)], axis=axis)
    minus = jnp.concatenate([cut(minus, 0, h), add(cut(minus, h, 2 * h), down).astype(BF16)], axis=axis)
    return minus, plus


def on_device(
    patches, image_counts, image_seq, image_offset, segment_ids, norm_gain, w_up, grad_hidden
):
    tok, width = patches.shape
    n_dp, n_mp = lax.axis_size("dp"), lax.axis_size("mp")
    full = width * n_mp
    half = w_up.shape[1] // 2
    me = lax.axis_index("dp")
    ring = jnp.array(RING, jnp.int32) + SIDE
    order = ((me // SIDE + ring[None, :]) % SIDE * SIDE + (me % SIDE + ring[:, None]) % SIDE).reshape(-1)

    sent = pl.pallas_call(
        route_kernel,
        in_specs=[HBM] * 2,
        out_specs=VMEM,
        out_shape=jax.ShapeDtypeStruct((n_dp * SLOT, width), BF16),
        scratch_shapes=[
            pltpu.VMEM((n_dp * SLOT, tok), BF16),
            pltpu.SMEM((3, image_counts.shape[0]), jnp.int32),
            pltpu.VMEM(patches.shape, BF16),
            pltpu.SemaphoreType.DMA((2,)),
        ],
        compiler_params=WIDE,
    )(jnp.stack([image_counts, image_seq, image_offset]), patches)
    wa = [w_up[:, :half]]
    wb = [w_up[:, half:]]
    wa += [move(wa[0], along_x(1)), move(wa[0], along_x(-1))]
    wb += [move(wb[0], along_y(1)), move(wb[0], along_y(-1))]
    got = lax.all_to_all(sent, "dp", split_axis=0, concat_axis=0, tiled=True)
    mine = pl.pallas_call(
        place_kernel,
        in_specs=[VMEM, VMEM],
        out_specs=VMEM,
        out_shape=jax.ShapeDtypeStruct((tok + 16, width), BF16),
        scratch_shapes=[pltpu.VMEM((n_dp * SLOT, tok), BF16)],
        compiler_params=ROOM,
    )(got, norm_gain.reshape(1, width))
    gathered = lax.all_gather(mine, "mp", axis=0)
    wa = spread(wa, along_x, along_y)
    wb = spread(wb, along_y, along_x)

    live = jnp.broadcast_to((segment_ids.reshape(tok, 1) >= 0).astype(F32), (tok, 128))
    normed, rows = norm(order, gathered, tok)
    row_mean, inverse_std = rows[0, 0:1], rows[1, 0:1]
    gelu_out, turned, terms, rows, *opposite = main(order, normed, wa, wb, grad_hidden, live)

    grad_normed = lax.psum_scatter(terms, "mp", scatter_dimension=0).astype(F32)

    plus, minus = part(normed, turned, 2, width), part(normed, turned, 1, width)
    a = ring_meet(minus[0], plus[0], *opposite[0:2], along_x, 1)
    b = ring_meet(minus[1], plus[1], *opposite[2:4], along_y, 1)
    a, b, normed, turned, rows = lax.optimization_barrier((a, b, normed, turned, rows))
    a = [move(a[0], along_x(-1)), move(a[1], along_x(1))]
    b = [move(b[0], along_y(-1)), move(b[1], along_y(1))]
    own = part(normed, turned, 0, width)
    a, b = add(own[0], *a), add(own[1], *b)

    def finish(x, along):
        cut = [x[:, q * width : (q + 1) * width] for q in range(SIDE)]
        sent = [c.astype(BF16) for c in cut[1:]]
        h = half // 2
        minus, plus = ring_meet(sent[0], sent[1], sent[2][:h], sent[2][h:], along, 0)
        return add(cut[0], move(minus, along(-1)), move(plus, along(1)))

    grad_scale = 1.0 / math.sqrt(tok * n_dp)
    grad_w = (jnp.concatenate([finish(a, along_y), finish(b, along_x)], axis=0) * grad_scale).T

    sums = lax.all_to_all(
        jnp.broadcast_to(rows[:, 0].reshape(1, 2 * tok), (n_mp, 2 * tok)),
        "mp",
        split_axis=0,
        concat_axis=0,
        tiled=True,
    )
    sums = jnp.sum(sums, axis=0, keepdims=True) / full
    first_mean, second_mean = sums[:, :tok], sums[:, tok:]

    scaled = (mine[:tok].T.astype(F32) - row_mean) * inverse_std
    grad_scaled = grad_normed * norm_gain.astype(F32)[:, None]
    grad_packed = inverse_std * (grad_scaled - first_mean - scaled * second_mean)
    gain_part = jnp.sum(grad_normed * scaled, axis=1)[None, :]
    gain_part = lax.all_to_all(
        jnp.broadcast_to(gain_part, (n_dp, width)), "dp", split_axis=0, concat_axis=0, tiled=True
    )
    grad_gain = jnp.sum(gain_part, axis=0) * grad_scale
    return (gelu_out, grad_w, grad_gain, grad_packed.astype(BF16).T)


def solution(mesh):
    return jax.shard_map(
        on_device,
        mesh=mesh,
        in_specs=(
            P("dp", "mp"),
            P("dp"),
            P("dp"),
            P("dp"),
            P("dp", None),
            P("mp"),
            P("dp", "mp"),
            P("dp", "mp"),
        ),
        out_specs=(P("dp", "mp"), P("dp", "mp"), P("mp"), P("dp", "mp")),
        check_vma=False,
    )
```

```python
import math

import jax
import jax.numpy as jnp
from jax import lax
from jax.experimental import pallas as pl
from jax.experimental.pallas import tpu as pltpu
from jax.sharding import PartitionSpec as P

SEQ_LEN = 128
SEQ_DEV = 4
IMG_MAX = 32
SLOT = 48

EPSILON = 1e-06
INV_ROOT2 = 0.7071067811865476
INV_ROOT_TWO_PI = 0.3989422804014327
BF16 = jnp.bfloat16
F32 = jnp.float32
VMEM = pl.BlockSpec(memory_space=pltpu.VMEM)
SMEM = pl.BlockSpec(memory_space=pltpu.SMEM)
HBM = pl.BlockSpec(memory_space=pltpu.HBM)
WIDE = pltpu.CompilerParams(vmem_limit_bytes=53 * 1024 * 1024)
FULL = pltpu.CompilerParams(vmem_limit_bytes=60 * 1024 * 1024)
ROOM = pltpu.CompilerParams(vmem_limit_bytes=12 * 1024 * 1024)
SIDE = 4
RING = (0, -1, 1, 2)
STEP = 16
NORM_FLOPS = 5 * 10**9
JOIN_FLOPS = 45 * 10**9


def dot(a, b, ca, cb):
    return lax.dot_general(a, b, (((ca,), (cb,)), ((), ())), preferred_element_type=F32)


def route_kernel(tables_in, patches_in, out, pick, tables, patches, sem):
    loads = [
        pltpu.make_async_copy(tables_in, tables, sem.at[0]),
        pltpu.make_async_copy(patches_in, patches, sem.at[1]),
    ]
    for load in loads:
        load.start()
    for load in loads:
        load.wait()
    counts, seqs, offsets = [[tables[k, i] for i in range(tables.shape[1])] for k in range(3)]
    n_img = len(counts)
    tok = patches.shape[0]
    rows = lax.broadcasted_iota(jnp.int32, (SLOT, tok), 0)
    cols = lax.broadcasted_iota(jnp.int32, (SLOT, tok), 1)
    start = jnp.int32(0)
    for i in range(n_img):
        at = pl.multiple_of(seqs[i] // SEQ_DEV * SLOT, SLOT)
        hit = (cols == rows + start) & (rows < counts[i])
        pick[pl.ds(at, SLOT), :] = jnp.where(hit, 1.0, 0.0).astype(BF16)
        start = start + counts[i]
    out[...] = dot(pick[...], patches[...], 1, 0).astype(BF16)
    tail = SLOT - IMG_MAX
    line = lax.broadcasted_iota(jnp.int32, (tail, patches.shape[1]), 0)
    for i in range(n_img):
        at = pl.multiple_of(seqs[i] // SEQ_DEV * SLOT + IMG_MAX, 16)
        place = seqs[i] % SEQ_DEV * SEQ_LEN + offsets[i]
        mark = jnp.where(line == 0, place // 256, jnp.where(line == 1, place % 256, counts[i]))
        out[pl.ds(at, tail), :] = mark.astype(F32).astype(BF16)


def place_kernel(got, gain, out, pick):
    n = got.shape[0] // SLOT
    tok = pick.shape[1]
    rows = lax.broadcasted_iota(jnp.int32, (SLOT, tok), 0).astype(F32)
    ahead = lax.broadcasted_iota(jnp.int32, (SLOT, tok), 1).astype(F32) - rows
    for i in range(n):
        mark = got[i * SLOT + IMG_MAX : (i + 1) * SLOT, 0:128].astype(F32)
        place = jnp.concatenate([mark[0:1] * 256.0 + mark[1:2]] * (tok // 128), axis=1)
        count = jnp.concatenate([mark[2:3]] * (tok // 128), axis=1)
        hit = (ahead == place) & (rows < count)
        pick[i * SLOT : (i + 1) * SLOT, :] = jnp.where(hit, 1.0, 0.0).astype(BF16)
    out[0:tok, :] = dot(pick[...], got[...], 0, 0).astype(BF16)
    out[tok : tok + 16, :] = jnp.broadcast_to(gain[...].astype(F32), (16, gain.shape[1])).astype(BF16)


def norm_kernel(order, rows_in, normed_out, row_out, xs, normed, cols, gains, sem_x, sem_out):
    n, rows, width = rows_in.shape
    tok = row_out.shape[2]
    full = n * width
    chunk = tok // 4
    loads = []
    for k in range(5):
        part = pl.ds(k * chunk, chunk if k < 4 else rows - tok)
        loads.append(pltpu.make_async_copy(rows_in.at[:, part, :], xs.at[:, part, :], sem_x.at[k]))
    for k in (4, 0, 1, 2, 3):
        loads[k].start()

    saves = [pltpu.make_async_copy(normed.at[pl.ds(tok, rows - tok), :], normed_out.at[pl.ds(tok, rows - tok), :], sem_out.at[4])]
    loads[4].wait()
    for p in range(n):
        gain = xs[order[p], tok:, :]
        gains[p] = gain.astype(F32)[0:8]
        normed[tok:, p * width : (p + 1) * width] = gain
    saves[0].start()
    for k in range(4):
        loads[k].wait()

        def sums(r, carry):
            here = pl.ds(pl.multiple_of(k * chunk + r * STEP, STEP), STEP)
            total = [jnp.zeros((STEP, 128), F32)] * 3
            squares = [jnp.zeros((STEP, 128), F32)] * 3
            for i in range(n):
                for c in range(width // 128):
                    x = xs[i, here, c * 128 : (c + 1) * 128].astype(F32)
                    total[c % 3] += x
                    squares[c % 3] += x * x
            cols[0, here, :] = total[0] + total[1] + total[2]
            cols[1, here, :] = squares[0] + squares[1] + squares[2]
            return carry

        lax.fori_loop(0, chunk // STEP, sums, 0)
        here = slice(k * chunk, (k + 1) * chunk)
        mean = jnp.sum(cols[0, here, :], axis=1, keepdims=True) / full
        var = jnp.sum(cols[1, here, :], axis=1, keepdims=True) / full - mean * mean
        cols[0, here, :] = jnp.broadcast_to(mean, (chunk, 128))
        cols[1, here, :] = jnp.broadcast_to(lax.rsqrt(var + EPSILON), (chunk, 128))

        def scale(r, carry):
            here = pl.ds(pl.multiple_of(k * chunk + r * STEP, STEP), STEP)
            mean = jnp.concatenate([cols[0, here, :]] * (width // 128), axis=1)
            inv = jnp.concatenate([cols[1, here, :]] * (width // 128), axis=1)
            for p in range(n):
                gain = jnp.broadcast_to(gains[p, 0:1, :], (STEP, width))
                x = (xs[order[p], here, :].astype(F32) - mean) * inv * gain
                normed[here, p * width : (p + 1) * width] = x.astype(BF16)
            return carry

        lax.fori_loop(0, chunk // STEP, scale, 0)
        part = pl.ds(k * chunk, chunk)
        saves.append(pltpu.make_async_copy(normed.at[part, :], normed_out.at[part, :], sem_out.at[k]))
        saves[-1].start()
    for k in range(2):
        row_out[k] = cols[k].T[0:8]
    for save in saves:
        save.wait()


def norm(order, gathered, tok):
    n, rows, width = gathered.shape
    return pl.pallas_call(
        norm_kernel,
        in_specs=[SMEM, HBM],
        out_specs=[HBM, VMEM],
        out_shape=[
            jax.ShapeDtypeStruct((rows, n * width), BF16),
            jax.ShapeDtypeStruct((2, 8, tok), F32),
        ],
        scratch_shapes=[
            pltpu.VMEM((n, rows, width), BF16),
            pltpu.VMEM((rows, n * width), BF16),
            pltpu.VMEM((2, tok, 128), F32),
            pltpu.VMEM((n, 8, width), F32),
            pltpu.SemaphoreType.DMA((5,)),
            pltpu.SemaphoreType.DMA((5,)),
        ],
        compiler_params=WIDE,
        cost_estimate=pl.CostEstimate(
            flops=NORM_FLOPS, bytes_accessed=4 * n * rows * width, transcendentals=0
        ),
    )(order, gathered)


def main_kernel(order, normed_in, *refs):
    pieces = refs[0:16]
    grad_hidden, live = refs[16:18]
    gelu_out, turned, dx_out, row_out = refs[18:22]
    a_up, a_down, b_up, b_down = refs[22:26]
    normed, w, hidden, grad_in, dx, cols, sem_w, sem_n, sem_dx = refs[26:]
    n, width, tok = dx_out.shape
    rows = normed_in.shape[0]
    units = grad_hidden.shape[1]
    half = units // 2
    loads = [pltpu.make_async_copy(piece, w.at[k], sem_w.at[k]) for k, piece in enumerate(pieces)]
    quarter = SIDE * width
    loads_n = []
    for q in range(SIDE):
        part = (slice(None), pl.ds(q * quarter, quarter))
        loads_n.append(pltpu.make_async_copy(normed_in.at[part], normed.at[part], sem_n.at[q]))
    queue = [load for q in range(SIDE) for load in (loads_n[q], loads[2 * q], loads[2 * q + 1])] + loads[8:]
    for load in queue[:6]:
        load.start()
    later = queue[6:]

    def arrived(load):
        load.wait()
        if later:
            later.pop(0).start()

    def features(places, count):
        return jnp.concatenate([normed[0:count, p * width : (p + 1) * width] for p in places], axis=1)

    def weight_rows(s, q, j, count):
        return w[8 * s + 2 * q + j // 2, j % 2 * width : (j % 2 + count) * width, :]

    for s in range(2):
        total = None
        for q in range(SIDE):
            for j in (0, 2):
                if s == 0 and j == 0:
                    arrived(loads_n[q])
                arrived(loads[8 * s + 2 * q + j // 2])
                places = [q * SIDE + j + e if s == 0 else (j + e) * SIDE + q for e in (0, 1)]
                term = dot(features(places, rows), weight_rows(s, q, j, 2), 1, 0)
                total = term if total is None else total + term
        hidden[:, s * half : (s + 1) * half] = total

    def epilogue(r, carry):
        here = pl.ds(pl.multiple_of(r * STEP, STEP), STEP)
        h = hidden[here, :]
        cdf = 0.5 * (1.0 + lax.erf(h * INV_ROOT2))
        gelu_out[here, :] = (h * cdf).astype(BF16)
        slope = cdf + h * jnp.exp(-0.5 * h * h) * INV_ROOT_TWO_PI
        lives = jnp.concatenate([live[here, :]] * (units // 128), axis=1)
        g = (grad_hidden[here, :].astype(F32) * slope * lives).astype(BF16)
        grad_in[here, :] = g
        g = g.astype(F32)
        gained = g * hidden[tok : tok + 1, :]
        cols[0, here, :] = jnp.broadcast_to(jnp.sum(gained, axis=1, keepdims=True), (STEP, 128))
        cols[1, here, :] = jnp.broadcast_to(jnp.sum(g * h, axis=1, keepdims=True), (STEP, 128))
        return carry

    lax.fori_loop(0, tok // STEP, epilogue, 0)
    turned[...] = grad_in[...].T
    for k in range(2):
        row_out[k] = cols[k].T[0:8]

    saves = []
    for q in range(SIDE):
        for j in (0, 2):
            first = weight_rows(0, q, j, 2)
            second = jnp.concatenate([weight_rows(1, j + e, q, 1) for e in (0, 1)], axis=0)
            term = dot(jnp.concatenate([first, second], axis=1), turned[...], 1, 0).astype(BF16)
            for e in (0, 1):
                p = q * SIDE + j + e
                dx[p] = term[e * width : (e + 1) * width, :]
                saves.append(pltpu.make_async_copy(dx.at[p], dx_out.at[order[p]], sem_dx.at[p]))
                saves[-1].start()

    last = SIDE - 1
    for j, (a_out, b_out) in enumerate(((a_up, b_up), (a_down, b_down))):
        a = features([2 * j * SIDE + last, (2 * j + 1) * SIDE + last], tok)
        a_out[...] = dot(turned[0:half, :], a, 1, 0).astype(BF16)
        b = features([last * SIDE + 2 * j, last * SIDE + 2 * j + 1], tok)
        b_out[...] = dot(turned[half:, :], b, 1, 0).astype(BF16)
    for copy in saves:
        copy.wait()


def main(order, normed, wa, wb, grad_hidden, live):
    n, (rows, full) = order.shape[0], normed.shape
    tok, units = grad_hidden.shape
    shape = jax.ShapeDtypeStruct
    return pl.pallas_call(
        main_kernel,
        in_specs=[SMEM] + [HBM] * 17 + [VMEM, VMEM],
        out_specs=[VMEM, VMEM, HBM] + [VMEM] * 5,
        out_shape=[
            shape((tok, units), BF16),
            shape((units, tok), BF16),
            shape((n, full // n, tok), BF16),
            shape((2, 8, tok), F32),
        ]
        + [shape((units // 2, 2 * full // n), BF16)] * 4,
        scratch_shapes=[
            pltpu.VMEM((rows, full), BF16),
            pltpu.VMEM((n, 2 * full // n, units // 2), BF16),
            pltpu.VMEM((rows, units), F32),
            pltpu.VMEM((tok, units), BF16),
            pltpu.VMEM((n, full // n, tok), BF16),
            pltpu.VMEM((2, tok, 128), F32),
            pltpu.SemaphoreType.DMA((n,)),
            pltpu.SemaphoreType.DMA((SIDE,)),
            pltpu.SemaphoreType.DMA((n,)),
        ],
        compiler_params=FULL,
        cost_estimate=pl.CostEstimate(
            flops=4 * tok * units * full, bytes_accessed=40 * 2**20, transcendentals=0
        ),
    )(order, normed, *wa, *wb, grad_hidden, live)


def part_kernel(turned, c0, c1, c2, c3, b, *outs):
    n = len(outs) // 2
    half, size = outs[0].shape
    for k in range(n):
        a = jnp.concatenate([c[...] for c in (c0, c1, c2, c3)[k * SIDE // n : (k + 1) * SIDE // n]], axis=1)
        outs[k][...] = dot(turned[0:half, :], a, 1, 0).astype(BF16)
        right = b[:, k * size : (k + 1) * size]
        outs[n + k][...] = dot(turned[half:, :], right, 1, 0).astype(BF16)


def part(normed, turned, q, width):
    units, tok = turned.shape
    half = units // 2
    n = 1
    cut = [pl.BlockSpec((tok, width), lambda i, j=j: (0, j * SIDE + q)) for j in range(SIDE)]
    out = (half, SIDE // n * width)
    return pl.pallas_call(
        part_kernel,
        grid=(1,),
        in_specs=[pl.BlockSpec((units, tok), lambda i: (0, 0))]
        + cut
        + [pl.BlockSpec((tok, SIDE * width), lambda i: (0, q))],
        out_specs=[pl.BlockSpec(out, lambda i: (0, 0))] * (2 * n),
        out_shape=[jax.ShapeDtypeStruct(out, BF16)] * (2 * n),
        compiler_params=ROOM,
        cost_estimate=pl.CostEstimate(
            flops=2 * tok * units * SIDE * width, bytes_accessed=8 * 2**20, transcendentals=0
        ),
    )(turned, normed, normed, normed, normed, normed)


def along_x(s):
    return [(i, (i // SIDE + s) % SIDE * SIDE + i % SIDE) for i in range(SIDE * SIDE)]


def along_y(s):
    return [(i, i // SIDE * SIDE + (i % SIDE + s) % SIDE) for i in range(SIDE * SIDE)]


def move(x, path):
    return lax.ppermute(x, "dp", path)


def add(*xs):
    return sum(x.astype(F32) for x in xs)


def opposite_halves(ring, along):
    own, below, above = ring
    h = own.shape[0] // 2
    return [move(below[:h], along(1)), move(above[h:], along(-1))]


def join_kernel(*refs):
    at = 0
    for piece in refs[:-1]:
        refs[-1][at : at + piece.shape[0], :] = piece[...]
        at += piece.shape[0]


def join(pieces):
    rows, cols = sum(x.shape[0] for x in pieces), pieces[0].shape[1]
    return pl.pallas_call(
        join_kernel,
        in_specs=[VMEM] * len(pieces),
        out_specs=VMEM,
        out_shape=jax.ShapeDtypeStruct((rows, cols), BF16),
        compiler_params=ROOM,
        cost_estimate=pl.CostEstimate(flops=JOIN_FLOPS, bytes_accessed=4 * rows * cols, transcendentals=0),
    )(*pieces)


def spread(ring, low, along, other):
    high = join([ring[2]] + opposite_halves(ring, along))
    low = [low, move(low, other(1)), move(low, other(-1))]
    high = [high, move(high, other(1)), move(high, other(-1))]
    low.append(move(low[1], other(1)))
    high.append(move(high[2], other(-1)))
    return [x for pair in zip(low, high) for x in pair]


def ring_meet(minus, plus, up, down, along, axis):
    h = up.shape[axis]
    cut = lambda x, a, b: lax.slice_in_dim(x, a, b, axis=axis)
    up, down = move(up, along(1)), move(down, along(-1))
    plus = jnp.concatenate([add(cut(plus, 0, h), up).astype(BF16), cut(plus, h, 2 * h)], axis=axis)
    minus = jnp.concatenate([cut(minus, 0, h), add(cut(minus, h, 2 * h), down).astype(BF16)], axis=axis)
    return minus, plus


def on_device(
    patches, image_counts, image_seq, image_offset, segment_ids, norm_gain, w_up, grad_hidden
):
    tok, width = patches.shape
    n_dp, n_mp = lax.axis_size("dp"), lax.axis_size("mp")
    full = width * n_mp
    half = w_up.shape[1] // 2
    me = lax.axis_index("dp")
    ring = jnp.array(RING, jnp.int32) + SIDE
    order = ((me // SIDE + ring[None, :]) % SIDE * SIDE + (me % SIDE + ring[:, None]) % SIDE).reshape(-1)

    sent = pl.pallas_call(
        route_kernel,
        in_specs=[HBM] * 2,
        out_specs=VMEM,
        out_shape=jax.ShapeDtypeStruct((n_dp * SLOT, width), BF16),
        scratch_shapes=[
            pltpu.VMEM((n_dp * SLOT, tok), BF16),
            pltpu.SMEM((3, image_counts.shape[0]), jnp.int32),
            pltpu.VMEM(patches.shape, BF16),
            pltpu.SemaphoreType.DMA((2,)),
        ],
        compiler_params=WIDE,
    )(jnp.stack([image_counts, image_seq, image_offset]), patches)
    wa = [w_up[:, :half]]
    wb = [w_up[:, half:]]
    wa += [move(wa[0], along_x(1)), move(wa[0], along_x(-1))]
    wb += [move(wb[0], along_y(1)), move(wb[0], along_y(-1))]
    got = lax.all_to_all(sent, "dp", split_axis=0, concat_axis=0, tiled=True)
    mine = pl.pallas_call(
        place_kernel,
        in_specs=[VMEM, VMEM],
        out_specs=VMEM,
        out_shape=jax.ShapeDtypeStruct((tok + 16, width), BF16),
        scratch_shapes=[pltpu.VMEM((n_dp * SLOT, tok), BF16)],
        compiler_params=ROOM,
    )(got, norm_gain.reshape(1, width))
    gathered = lax.all_gather(mine, "mp", axis=0)
    live = jnp.broadcast_to((segment_ids.reshape(tok, 1) >= 0).astype(F32), (tok, 128))
    wa, wb, low_a, low_b, live = lax.optimization_barrier((wa, wb, join(wa[:2]), join(wb[:2]), live))
    wa = spread(wa, low_a, along_x, along_y)
    wb = spread(wb, low_b, along_y, along_x)

    normed, rows = norm(order, gathered, tok)
    row_mean, inverse_std = rows[0, 0:1], rows[1, 0:1]
    gelu_out, turned, terms, rows, *opposite = main(order, normed, wa, wb, grad_hidden, live)

    grad_normed = lax.psum_scatter(terms, "mp", scatter_dimension=0).astype(F32)

    plus, minus = part(normed, turned, 2, width), part(normed, turned, 1, width)
    a = ring_meet(minus[0], plus[0], *opposite[0:2], along_x, 1)
    b = ring_meet(minus[1], plus[1], *opposite[2:4], along_y, 1)
    a, b, normed, turned, rows = lax.optimization_barrier((a, b, normed, turned, rows))
    a = [move(a[0], along_x(-1)), move(a[1], along_x(1))]
    b = [move(b[0], along_y(-1)), move(b[1], along_y(1))]
    own = part(normed, turned, 0, width)
    a, b = add(own[0], *a), add(own[1], *b)

    def finish(x, along):
        cut = [x[:, q * width : (q + 1) * width] for q in range(SIDE)]
        sent = [c.astype(BF16) for c in cut[1:]]
        h = half // 2
        minus, plus = ring_meet(sent[0], sent[1], sent[2][:h], sent[2][h:], along, 0)
        return add(cut[0], move(minus, along(-1)), move(plus, along(1)))

    grad_scale = 1.0 / math.sqrt(tok * n_dp)
    grad_w = (jnp.concatenate([finish(a, along_y), finish(b, along_x)], axis=0) * grad_scale).T

    sums = lax.all_to_all(
        jnp.broadcast_to(rows[:, 0].reshape(1, 2 * tok), (n_mp, 2 * tok)),
        "mp",
        split_axis=0,
        concat_axis=0,
        tiled=True,
    )
    sums = jnp.sum(sums, axis=0, keepdims=True) / full
    first_mean, second_mean = sums[:, :tok], sums[:, tok:]

    scaled = (mine[:tok].T.astype(F32) - row_mean) * inverse_std
    grad_scaled = grad_normed * norm_gain.astype(F32)[:, None]
    grad_packed = inverse_std * (grad_scaled - first_mean - scaled * second_mean)
    gain_part = jnp.sum(grad_normed * scaled, axis=1)[None, :]
    gain_part = lax.all_to_all(
        jnp.broadcast_to(gain_part, (n_dp, width)), "dp", split_axis=0, concat_axis=0, tiled=True
    )
    grad_gain = jnp.sum(gain_part, axis=0) * grad_scale
    return (gelu_out, grad_w, grad_gain, grad_packed.astype(BF16).T)


def solution(mesh):
    return jax.shard_map(
        on_device,
        mesh=mesh,
        in_specs=(
            P("dp", "mp"),
            P("dp"),
            P("dp"),
            P("dp"),
            P("dp", None),
            P("mp"),
            P("dp", "mp"),
            P("dp", "mp"),
        ),
        out_specs=(P("dp", "mp"), P("dp", "mp"), P("mp"), P("dp", "mp")),
        check_vma=False,
    )
```

```python
import math

import jax
import jax.numpy as jnp
from jax import lax
from jax.experimental import pallas as pl
from jax.experimental.pallas import tpu as pltpu
from jax.sharding import PartitionSpec as P

SEQ_LEN = 128
SEQ_DEV = 4
IMG_MAX = 32
SLOT = 48

EPSILON = 1e-06
INV_ROOT2 = 0.7071067811865476
INV_ROOT_TWO_PI = 0.3989422804014327
BF16 = jnp.bfloat16
F32 = jnp.float32
VMEM = pl.BlockSpec(memory_space=pltpu.VMEM)
SMEM = pl.BlockSpec(memory_space=pltpu.SMEM)
HBM = pl.BlockSpec(memory_space=pltpu.HBM)
WIDE = pltpu.CompilerParams(vmem_limit_bytes=53 * 1024 * 1024)
FULL = pltpu.CompilerParams(vmem_limit_bytes=60 * 1024 * 1024)
ROOM = pltpu.CompilerParams(vmem_limit_bytes=12 * 1024 * 1024)
SIDE = 4
RING = (0, -1, 1, 2)
STEP = 32
NORM_FLOPS = 5 * 10**9
JOIN_FLOPS = 45 * 10**9


def dot(a, b, ca, cb):
    return lax.dot_general(a, b, (((ca,), (cb,)), ((), ())), preferred_element_type=F32)


def route_kernel(tables_in, patches_in, out, pick, tables, patches, sem):
    loads = [
        pltpu.make_async_copy(tables_in, tables, sem.at[0]),
        pltpu.make_async_copy(patches_in, patches, sem.at[1]),
    ]
    for load in loads:
        load.start()
    for load in loads:
        load.wait()
    counts, seqs, offsets = [[tables[k, i] for i in range(tables.shape[1])] for k in range(3)]
    n_img = len(counts)
    tok = patches.shape[0]
    rows = lax.broadcasted_iota(jnp.int32, (SLOT, tok), 0)
    cols = lax.broadcasted_iota(jnp.int32, (SLOT, tok), 1)
    start = jnp.int32(0)
    for i in range(n_img):
        at = pl.multiple_of(seqs[i] // SEQ_DEV * SLOT, SLOT)
        hit = (cols == rows + start) & (rows < counts[i])
        pick[pl.ds(at, SLOT), :] = jnp.where(hit, 1.0, 0.0).astype(BF16)
        start = start + counts[i]
    out[...] = dot(pick[...], patches[...], 1, 0).astype(BF16)
    tail = SLOT - IMG_MAX
    line = lax.broadcasted_iota(jnp.int32, (tail, patches.shape[1]), 0)
    for i in range(n_img):
        at = pl.multiple_of(seqs[i] // SEQ_DEV * SLOT + IMG_MAX, 16)
        place = seqs[i] % SEQ_DEV * SEQ_LEN + offsets[i]
        mark = jnp.where(line == 0, place // 256, jnp.where(line == 1, place % 256, counts[i]))
        out[pl.ds(at, tail), :] = mark.astype(F32).astype(BF16)


def place_kernel(got, gain, out, pick):
    n = got.shape[0] // SLOT
    tok = pick.shape[1]
    rows = lax.broadcasted_iota(jnp.int32, (SLOT, tok), 0).astype(F32)
    ahead = lax.broadcasted_iota(jnp.int32, (SLOT, tok), 1).astype(F32) - rows
    for i in range(n):
        mark = got[i * SLOT + IMG_MAX : (i + 1) * SLOT, 0:128].astype(F32)
        place = jnp.concatenate([mark[0:1] * 256.0 + mark[1:2]] * (tok // 128), axis=1)
        count = jnp.concatenate([mark[2:3]] * (tok // 128), axis=1)
        hit = (ahead == place) & (rows < count)
        pick[i * SLOT : (i + 1) * SLOT, :] = jnp.where(hit, 1.0, 0.0).astype(BF16)
    out[0:tok, :] = dot(pick[...], got[...], 0, 0).astype(BF16)
    out[tok : tok + 16, :] = jnp.broadcast_to(gain[...].astype(F32), (16, gain.shape[1])).astype(BF16)


def norm_kernel(order, rows_in, normed_out, row_out, xs, normed, cols, gains, sem_x, sem_out):
    n, rows, width = rows_in.shape
    tok = row_out.shape[2]
    full = n * width
    chunk = tok // 4
    loads = []
    for k in range(5):
        part = pl.ds(k * chunk, chunk if k < 4 else rows - tok)
        loads.append(pltpu.make_async_copy(rows_in.at[:, part, :], xs.at[:, part, :], sem_x.at[k]))
    for k in (4, 0, 1, 2, 3):
        loads[k].start()

    saves = [pltpu.make_async_copy(normed.at[pl.ds(tok, rows - tok), :], normed_out.at[pl.ds(tok, rows - tok), :], sem_out.at[4])]
    loads[4].wait()
    for p in range(n):
        gain = xs[order[p], tok:, :]
        gains[p] = gain.astype(F32)[0:8]
        normed[tok:, p * width : (p + 1) * width] = gain
    saves[0].start()
    for k in range(4):
        loads[k].wait()

        def sums(r, carry):
            here = pl.ds(pl.multiple_of(k * chunk + r * STEP, STEP), STEP)
            total = [jnp.zeros((STEP, 128), F32)] * 3
            squares = [jnp.zeros((STEP, 128), F32)] * 3
            for i in range(n):
                for c in range(width // 128):
                    x = xs[i, here, c * 128 : (c + 1) * 128].astype(F32)
                    total[c % 3] += x
                    squares[c % 3] += x * x
            cols[0, here, :] = total[0] + total[1] + total[2]
            cols[1, here, :] = squares[0] + squares[1] + squares[2]
            return carry

        lax.fori_loop(0, chunk // STEP, sums, 0)
        here = slice(k * chunk, (k + 1) * chunk)
        mean = jnp.sum(cols[0, here, :], axis=1, keepdims=True) / full
        var = jnp.sum(cols[1, here, :], axis=1, keepdims=True) / full - mean * mean
        cols[0, here, :] = jnp.broadcast_to(mean, (chunk, 128))
        cols[1, here, :] = jnp.broadcast_to(lax.rsqrt(var + EPSILON), (chunk, 128))

        def scale(r, carry):
            here = pl.ds(pl.multiple_of(k * chunk + r * STEP, STEP), STEP)
            mean = jnp.concatenate([cols[0, here, :]] * (width // 128), axis=1)
            inv = jnp.concatenate([cols[1, here, :]] * (width // 128), axis=1)
            for p in range(n):
                gain = jnp.broadcast_to(gains[p, 0:1, :], (STEP, width))
                x = (xs[order[p], here, :].astype(F32) - mean) * inv * gain
                normed[here, p * width : (p + 1) * width] = x.astype(BF16)
            return carry

        lax.fori_loop(0, chunk // STEP, scale, 0)
        part = pl.ds(k * chunk, chunk)
        saves.append(pltpu.make_async_copy(normed.at[part, :], normed_out.at[part, :], sem_out.at[k]))
        saves[-1].start()
    for k in range(2):
        row_out[k] = cols[k].T[0:8]
    for save in saves:
        save.wait()


def norm(order, gathered, tok):
    n, rows, width = gathered.shape
    return pl.pallas_call(
        norm_kernel,
        in_specs=[SMEM, HBM],
        out_specs=[HBM, VMEM],
        out_shape=[
            jax.ShapeDtypeStruct((rows, n * width), BF16),
            jax.ShapeDtypeStruct((2, 8, tok), F32),
        ],
        scratch_shapes=[
            pltpu.VMEM((n, rows, width), BF16),
            pltpu.VMEM((rows, n * width), BF16),
            pltpu.VMEM((2, tok, 128), F32),
            pltpu.VMEM((n, 8, width), F32),
            pltpu.SemaphoreType.DMA((5,)),
            pltpu.SemaphoreType.DMA((5,)),
        ],
        compiler_params=WIDE,
        cost_estimate=pl.CostEstimate(
            flops=NORM_FLOPS, bytes_accessed=4 * n * rows * width, transcendentals=0
        ),
    )(order, gathered)


def main_kernel(order, normed_in, *refs):
    pieces = refs[0:16]
    grad_hidden, live = refs[16:18]
    gelu_out, turned, dx_out, row_out = refs[18:22]
    a_up, a_down, b_up, b_down = refs[22:26]
    normed, w, hidden, grad_in, dx, cols, sem_w, sem_n, sem_dx = refs[26:]
    n, width, tok = dx_out.shape
    rows = normed_in.shape[0]
    units = grad_hidden.shape[1]
    half = units // 2
    loads = [pltpu.make_async_copy(piece, w.at[k], sem_w.at[k]) for k, piece in enumerate(pieces)]
    quarter = SIDE * width
    loads_n = []
    for q in range(SIDE):
        part = (slice(None), pl.ds(q * quarter, quarter))
        loads_n.append(pltpu.make_async_copy(normed_in.at[part], normed.at[part], sem_n.at[q]))
    queue = [load for q in range(SIDE) for load in (loads_n[q], loads[2 * q], loads[2 * q + 1])] + loads[8:]
    for load in queue[:6]:
        load.start()
    later = queue[6:]

    def arrived(load):
        load.wait()
        if later:
            later.pop(0).start()

    def features(places, count):
        return jnp.concatenate([normed[0:count, p * width : (p + 1) * width] for p in places], axis=1)

    def weight_rows(s, q, j, count):
        return w[8 * s + 2 * q + j // 2, j % 2 * width : (j % 2 + count) * width, :]

    for s in range(2):
        total = None
        for q in range(SIDE):
            for j in (0, 2):
                if s == 0 and j == 0:
                    arrived(loads_n[q])
                arrived(loads[8 * s + 2 * q + j // 2])
                places = [q * SIDE + j + e if s == 0 else (j + e) * SIDE + q for e in (0, 1)]
                term = dot(features(places, rows), weight_rows(s, q, j, 2), 1, 0)
                total = term if total is None else total + term
        hidden[:, s * half : (s + 1) * half] = total

    def epilogue(r, carry):
        here = pl.ds(pl.multiple_of(r * STEP, STEP), STEP)
        h = hidden[here, :]
        cdf = 0.5 * (1.0 + lax.erf(h * INV_ROOT2))
        gelu_out[here, :] = (h * cdf).astype(BF16)
        slope = cdf + h * jnp.exp(-0.5 * h * h) * INV_ROOT_TWO_PI
        lives = jnp.concatenate([live[here, :]] * (units // 128), axis=1)
        g = (grad_hidden[here, :].astype(F32) * slope * lives).astype(BF16)
        grad_in[here, :] = g
        g = g.astype(F32)
        gained = g * hidden[tok : tok + 1, :]
        cols[0, here, :] = jnp.broadcast_to(jnp.sum(gained, axis=1, keepdims=True), (STEP, 128))
        cols[1, here, :] = jnp.broadcast_to(jnp.sum(g * h, axis=1, keepdims=True), (STEP, 128))
        return carry

    lax.fori_loop(0, tok // STEP, epilogue, 0)
    turned[...] = grad_in[...].T
    for k in range(2):
        row_out[k] = cols[k].T[0:8]

    saves = []
    for q in range(SIDE):
        for j in (0, 2):
            first = weight_rows(0, q, j, 2)
            second = jnp.concatenate([weight_rows(1, j + e, q, 1) for e in (0, 1)], axis=0)
            term = dot(jnp.concatenate([first, second], axis=1), turned[...], 1, 0).astype(BF16)
            for e in (0, 1):
                p = q * SIDE + j + e
                dx[p] = term[e * width : (e + 1) * width, :]
                saves.append(pltpu.make_async_copy(dx.at[p], dx_out.at[order[p]], sem_dx.at[p]))
                saves[-1].start()

    last = SIDE - 1
    for j, (a_out, b_out) in enumerate(((a_up, b_up), (a_down, b_down))):
        a = features([2 * j * SIDE + last, (2 * j + 1) * SIDE + last], tok)
        a_out[...] = dot(turned[0:half, :], a, 1, 0).astype(BF16)
        b = features([last * SIDE + 2 * j, last * SIDE + 2 * j + 1], tok)
        b_out[...] = dot(turned[half:, :], b, 1, 0).astype(BF16)
    for copy in saves:
        copy.wait()


def main(order, normed, wa, wb, grad_hidden, live):
    n, (rows, full) = order.shape[0], normed.shape
    tok, units = grad_hidden.shape
    shape = jax.ShapeDtypeStruct
    return pl.pallas_call(
        main_kernel,
        in_specs=[SMEM] + [HBM] * 17 + [VMEM, VMEM],
        out_specs=[VMEM, VMEM, HBM] + [VMEM] * 5,
        out_shape=[
            shape((tok, units), BF16),
            shape((units, tok), BF16),
            shape((n, full // n, tok), BF16),
            shape((2, 8, tok), F32),
        ]
        + [shape((units // 2, 2 * full // n), BF16)] * 4,
        scratch_shapes=[
            pltpu.VMEM((rows, full), BF16),
            pltpu.VMEM((n, 2 * full // n, units // 2), BF16),
            pltpu.VMEM((rows, units), F32),
            pltpu.VMEM((tok, units), BF16),
            pltpu.VMEM((n, full // n, tok), BF16),
            pltpu.VMEM((2, tok, 128), F32),
            pltpu.SemaphoreType.DMA((n,)),
            pltpu.SemaphoreType.DMA((SIDE,)),
            pltpu.SemaphoreType.DMA((n,)),
        ],
        compiler_params=FULL,
        cost_estimate=pl.CostEstimate(
            flops=4 * tok * units * full, bytes_accessed=40 * 2**20, transcendentals=0
        ),
    )(order, normed, *wa, *wb, grad_hidden, live)


def part_kernel(turned, c0, c1, c2, c3, b, *outs):
    n = len(outs) // 2
    half, size = outs[0].shape
    for k in range(n):
        a = jnp.concatenate([c[...] for c in (c0, c1, c2, c3)[k * SIDE // n : (k + 1) * SIDE // n]], axis=1)
        outs[k][...] = dot(turned[0:half, :], a, 1, 0).astype(BF16)
        right = b[:, k * size : (k + 1) * size]
        outs[n + k][...] = dot(turned[half:, :], right, 1, 0).astype(BF16)


def part(normed, turned, q, width):
    units, tok = turned.shape
    half = units // 2
    n = 1
    cut = [pl.BlockSpec((tok, width), lambda i, j=j: (0, j * SIDE + q)) for j in range(SIDE)]
    out = (half, SIDE // n * width)
    return pl.pallas_call(
        part_kernel,
        grid=(1,),
        in_specs=[pl.BlockSpec((units, tok), lambda i: (0, 0))]
        + cut
        + [pl.BlockSpec((tok, SIDE * width), lambda i: (0, q))],
        out_specs=[pl.BlockSpec(out, lambda i: (0, 0))] * (2 * n),
        out_shape=[jax.ShapeDtypeStruct(out, BF16)] * (2 * n),
        compiler_params=ROOM,
        cost_estimate=pl.CostEstimate(
            flops=2 * tok * units * SIDE * width, bytes_accessed=8 * 2**20, transcendentals=0
        ),
    )(turned, normed, normed, normed, normed, normed)


def along_x(s):
    return [(i, (i // SIDE + s) % SIDE * SIDE + i % SIDE) for i in range(SIDE * SIDE)]


def along_y(s):
    return [(i, i // SIDE * SIDE + (i % SIDE + s) % SIDE) for i in range(SIDE * SIDE)]


def move(x, path):
    return lax.ppermute(x, "dp", path)


def add(*xs):
    return sum(x.astype(F32) for x in xs)


def opposite_halves(ring, along):
    own, below, above = ring
    h = own.shape[0] // 2
    return [move(below[:h], along(1)), move(above[h:], along(-1))]


def join_kernel(*refs):
    at = 0
    for piece in refs[:-1]:
        refs[-1][at : at + piece.shape[0], :] = piece[...]
        at += piece.shape[0]


def join(pieces):
    rows, cols = sum(x.shape[0] for x in pieces), pieces[0].shape[1]
    return pl.pallas_call(
        join_kernel,
        in_specs=[VMEM] * len(pieces),
        out_specs=VMEM,
        out_shape=jax.ShapeDtypeStruct((rows, cols), BF16),
        compiler_params=ROOM,
        cost_estimate=pl.CostEstimate(flops=JOIN_FLOPS, bytes_accessed=4 * rows * cols, transcendentals=0),
    )(*pieces)


def spread(ring, low, along, other):
    high = join([ring[2]] + opposite_halves(ring, along))
    low = [low, move(low, other(1)), move(low, other(-1))]
    high = [high, move(high, other(1)), move(high, other(-1))]
    low.append(move(low[1], other(1)))
    high.append(move(high[2], other(-1)))
    return [x for pair in zip(low, high) for x in pair]


def ring_meet(minus, plus, up, down, along, axis):
    h = up.shape[axis]
    cut = lambda x, a, b: lax.slice_in_dim(x, a, b, axis=axis)
    up, down = move(up, along(1)), move(down, along(-1))
    plus = jnp.concatenate([add(cut(plus, 0, h), up).astype(BF16), cut(plus, h, 2 * h)], axis=axis)
    minus = jnp.concatenate([cut(minus, 0, h), add(cut(minus, h, 2 * h), down).astype(BF16)], axis=axis)
    return minus, plus


def on_device(
    patches, image_counts, image_seq, image_offset, segment_ids, norm_gain, w_up, grad_hidden
):
    tok, width = patches.shape
    n_dp, n_mp = lax.axis_size("dp"), lax.axis_size("mp")
    full = width * n_mp
    half = w_up.shape[1] // 2
    me = lax.axis_index("dp")
    ring = jnp.array(RING, jnp.int32) + SIDE
    order = ((me // SIDE + ring[None, :]) % SIDE * SIDE + (me % SIDE + ring[:, None]) % SIDE).reshape(-1)

    sent = pl.pallas_call(
        route_kernel,
        in_specs=[HBM] * 2,
        out_specs=VMEM,
        out_shape=jax.ShapeDtypeStruct((n_dp * SLOT, width), BF16),
        scratch_shapes=[
            pltpu.VMEM((n_dp * SLOT, tok), BF16),
            pltpu.SMEM((3, image_counts.shape[0]), jnp.int32),
            pltpu.VMEM(patches.shape, BF16),
            pltpu.SemaphoreType.DMA((2,)),
        ],
        compiler_params=WIDE,
    )(jnp.stack([image_counts, image_seq, image_offset]), patches)
    wa = [w_up[:, :half]]
    wb = [w_up[:, half:]]
    wa += [move(wa[0], along_x(1)), move(wa[0], along_x(-1))]
    wb += [move(wb[0], along_y(1)), move(wb[0], along_y(-1))]
    got = lax.all_to_all(sent, "dp", split_axis=0, concat_axis=0, tiled=True)
    mine = pl.pallas_call(
        place_kernel,
        in_specs=[VMEM, VMEM],
        out_specs=VMEM,
        out_shape=jax.ShapeDtypeStruct((tok + 16, width), BF16),
        scratch_shapes=[pltpu.VMEM((n_dp * SLOT, tok), BF16)],
        compiler_params=ROOM,
    )(got, norm_gain.reshape(1, width))
    gathered = lax.all_gather(mine, "mp", axis=0)
    live = jnp.broadcast_to((segment_ids.reshape(tok, 1) >= 0).astype(F32), (tok, 128))
    wa, wb, low_a, low_b, live = lax.optimization_barrier((wa, wb, join(wa[:2]), join(wb[:2]), live))
    wa = spread(wa, low_a, along_x, along_y)
    wb = spread(wb, low_b, along_y, along_x)

    normed, rows = norm(order, gathered, tok)
    row_mean, inverse_std = rows[0, 0:1], rows[1, 0:1]
    gelu_out, turned, terms, rows, *opposite = main(order, normed, wa, wb, grad_hidden, live)

    grad_normed = lax.psum_scatter(terms, "mp", scatter_dimension=0).astype(F32)

    plus, minus = part(normed, turned, 2, width), part(normed, turned, 1, width)
    a = ring_meet(minus[0], plus[0], *opposite[0:2], along_x, 1)
    b = ring_meet(minus[1], plus[1], *opposite[2:4], along_y, 1)
    a, b, normed, turned, rows = lax.optimization_barrier((a, b, normed, turned, rows))
    a = [move(a[0], along_x(-1)), move(a[1], along_x(1))]
    b = [move(b[0], along_y(-1)), move(b[1], along_y(1))]
    own = part(normed, turned, 0, width)
    a, b = add(own[0], *a), add(own[1], *b)

    def finish(x, along):
        cut = [x[:, q * width : (q + 1) * width] for q in range(SIDE)]
        sent = [c.astype(BF16) for c in cut[1:]]
        h = half // 2
        minus, plus = ring_meet(sent[0], sent[1], sent[2][:h], sent[2][h:], along, 0)
        return add(cut[0], move(minus, along(-1)), move(plus, along(1)))

    grad_scale = 1.0 / math.sqrt(tok * n_dp)
    grad_w = (jnp.concatenate([finish(a, along_y), finish(b, along_x)], axis=0) * grad_scale).T

    sums = lax.all_to_all(
        jnp.broadcast_to(rows[:, 0].reshape(1, 2 * tok), (n_mp, 2 * tok)),
        "mp",
        split_axis=0,
        concat_axis=0,
        tiled=True,
    )
    sums = jnp.sum(sums, axis=0, keepdims=True) / full
    first_mean, second_mean = sums[:, :tok], sums[:, tok:]

    scaled = (mine[:tok].T.astype(F32) - row_mean) * inverse_std
    grad_scaled = grad_normed * norm_gain.astype(F32)[:, None]
    grad_packed = inverse_std * (grad_scaled - first_mean - scaled * second_mean)
    gain_part = jnp.sum(grad_normed * scaled, axis=1)[None, :]
    gain_part = lax.all_to_all(
        jnp.broadcast_to(gain_part, (n_dp, width)), "dp", split_axis=0, concat_axis=0, tiled=True
    )
    grad_gain = jnp.sum(gain_part, axis=0) * grad_scale
    return (gelu_out, grad_w, grad_gain, grad_packed.astype(BF16).T)


def solution(mesh):
    return jax.shard_map(
        on_device,
        mesh=mesh,
        in_specs=(
            P("dp", "mp"),
            P("dp"),
            P("dp"),
            P("dp"),
            P("dp", None),
            P("mp"),
            P("dp", "mp"),
            P("dp", "mp"),
        ),
        out_specs=(P("dp", "mp"), P("dp", "mp"), P("mp"), P("dp", "mp")),
        check_vma=False,
    )
```

```python
import math

import jax
import jax.numpy as jnp
from jax import lax
from jax.experimental import pallas as pl
from jax.experimental.pallas import tpu as pltpu
from jax.sharding import PartitionSpec as P

SEQ_LEN = 128
SEQ_DEV = 4
IMG_MAX = 32
SLOT = 48

EPSILON = 1e-06
INV_ROOT2 = 0.7071067811865476
INV_ROOT_TWO_PI = 0.3989422804014327
BF16 = jnp.bfloat16
F32 = jnp.float32
VMEM = pl.BlockSpec(memory_space=pltpu.VMEM)
SMEM = pl.BlockSpec(memory_space=pltpu.SMEM)
HBM = pl.BlockSpec(memory_space=pltpu.HBM)
WIDE = pltpu.CompilerParams(vmem_limit_bytes=53 * 1024 * 1024)
FULL = pltpu.CompilerParams(vmem_limit_bytes=60 * 1024 * 1024)
ROOM = pltpu.CompilerParams(vmem_limit_bytes=12 * 1024 * 1024)
SIDE = 4
RING = (0, -1, 1, 2)
STEP = 64
NORM_FLOPS = 5 * 10**9
JOIN_FLOPS = 45 * 10**9


def dot(a, b, ca, cb):
    return lax.dot_general(a, b, (((ca,), (cb,)), ((), ())), preferred_element_type=F32)


def route_kernel(tables_in, patches_in, out, pick, tables, patches, sem):
    loads = [
        pltpu.make_async_copy(tables_in, tables, sem.at[0]),
        pltpu.make_async_copy(patches_in, patches, sem.at[1]),
    ]
    for load in loads:
        load.start()
    for load in loads:
        load.wait()
    counts, seqs, offsets = [[tables[k, i] for i in range(tables.shape[1])] for k in range(3)]
    n_img = len(counts)
    tok = patches.shape[0]
    rows = lax.broadcasted_iota(jnp.int32, (SLOT, tok), 0)
    cols = lax.broadcasted_iota(jnp.int32, (SLOT, tok), 1)
    start = jnp.int32(0)
    for i in range(n_img):
        at = pl.multiple_of(seqs[i] // SEQ_DEV * SLOT, SLOT)
        hit = (cols == rows + start) & (rows < counts[i])
        pick[pl.ds(at, SLOT), :] = jnp.where(hit, 1.0, 0.0).astype(BF16)
        start = start + counts[i]
    out[...] = dot(pick[...], patches[...], 1, 0).astype(BF16)
    tail = SLOT - IMG_MAX
    line = lax.broadcasted_iota(jnp.int32, (tail, patches.shape[1]), 0)
    for i in range(n_img):
        at = pl.multiple_of(seqs[i] // SEQ_DEV * SLOT + IMG_MAX, 16)
        place = seqs[i] % SEQ_DEV * SEQ_LEN + offsets[i]
        mark = jnp.where(line == 0, place // 256, jnp.where(line == 1, place % 256, counts[i]))
        out[pl.ds(at, tail), :] = mark.astype(F32).astype(BF16)


def place_kernel(got, gain, out, pick):
    n = got.shape[0] // SLOT
    tok = pick.shape[1]
    rows = lax.broadcasted_iota(jnp.int32, (SLOT, tok), 0).astype(F32)
    ahead = lax.broadcasted_iota(jnp.int32, (SLOT, tok), 1).astype(F32) - rows
    for i in range(n):
        mark = got[i * SLOT + IMG_MAX : (i + 1) * SLOT, 0:128].astype(F32)
        place = jnp.concatenate([mark[0:1] * 256.0 + mark[1:2]] * (tok // 128), axis=1)
        count = jnp.concatenate([mark[2:3]] * (tok // 128), axis=1)
        hit = (ahead == place) & (rows < count)
        pick[i * SLOT : (i + 1) * SLOT, :] = jnp.where(hit, 1.0, 0.0).astype(BF16)
    out[0:tok, :] = dot(pick[...], got[...], 0, 0).astype(BF16)
    out[tok : tok + 16, :] = jnp.broadcast_to(gain[...].astype(F32), (16, gain.shape[1])).astype(BF16)


def norm_kernel(order, rows_in, normed_out, row_out, xs, normed, cols, gains, sem_x, sem_out):
    n, rows, width = rows_in.shape
    tok = row_out.shape[2]
    full = n * width
    chunk = tok // 4
    loads = []
    for k in range(5):
        part = pl.ds(k * chunk, chunk if k < 4 else rows - tok)
        loads.append(pltpu.make_async_copy(rows_in.at[:, part, :], xs.at[:, part, :], sem_x.at[k]))
    for k in (4, 0, 1, 2, 3):
        loads[k].start()

    saves = [pltpu.make_async_copy(normed.at[pl.ds(tok, rows - tok), :], normed_out.at[pl.ds(tok, rows - tok), :], sem_out.at[4])]
    loads[4].wait()
    for p in range(n):
        gain = xs[order[p], tok:, :]
        gains[p] = gain.astype(F32)[0:8]
        normed[tok:, p * width : (p + 1) * width] = gain
    saves[0].start()
    for k in range(4):
        loads[k].wait()

        def sums(r, carry):
            here = pl.ds(pl.multiple_of(k * chunk + r * STEP, STEP), STEP)
            total = [jnp.zeros((STEP, 128), F32)] * 3
            squares = [jnp.zeros((STEP, 128), F32)] * 3
            for i in range(n):
                for c in range(width // 128):
                    x = xs[i, here, c * 128 : (c + 1) * 128].astype(F32)
                    total[c % 3] += x
                    squares[c % 3] += x * x
            cols[0, here, :] = total[0] + total[1] + total[2]
            cols[1, here, :] = squares[0] + squares[1] + squares[2]
            return carry

        lax.fori_loop(0, chunk // STEP, sums, 0)
        here = slice(k * chunk, (k + 1) * chunk)
        mean = jnp.sum(cols[0, here, :], axis=1, keepdims=True) / full
        var = jnp.sum(cols[1, here, :], axis=1, keepdims=True) / full - mean * mean
        cols[0, here, :] = jnp.broadcast_to(mean, (chunk, 128))
        cols[1, here, :] = jnp.broadcast_to(lax.rsqrt(var + EPSILON), (chunk, 128))

        def scale(r, carry):
            here = pl.ds(pl.multiple_of(k * chunk + r * STEP, STEP), STEP)
            mean = jnp.concatenate([cols[0, here, :]] * (width // 128), axis=1)
            inv = jnp.concatenate([cols[1, here, :]] * (width // 128), axis=1)
            for p in range(n):
                gain = jnp.broadcast_to(gains[p, 0:1, :], (STEP, width))
                x = (xs[order[p], here, :].astype(F32) - mean) * inv * gain
                normed[here, p * width : (p + 1) * width] = x.astype(BF16)
            return carry

        lax.fori_loop(0, chunk // STEP, scale, 0)
        part = pl.ds(k * chunk, chunk)
        saves.append(pltpu.make_async_copy(normed.at[part, :], normed_out.at[part, :], sem_out.at[k]))
        saves[-1].start()
    for k in range(2):
        row_out[k] = cols[k].T[0:8]
    for save in saves:
        save.wait()


def norm(order, gathered, tok):
    n, rows, width = gathered.shape
    return pl.pallas_call(
        norm_kernel,
        in_specs=[SMEM, HBM],
        out_specs=[HBM, VMEM],
        out_shape=[
            jax.ShapeDtypeStruct((rows, n * width), BF16),
            jax.ShapeDtypeStruct((2, 8, tok), F32),
        ],
        scratch_shapes=[
            pltpu.VMEM((n, rows, width), BF16),
            pltpu.VMEM((rows, n * width), BF16),
            pltpu.VMEM((2, tok, 128), F32),
            pltpu.VMEM((n, 8, width), F32),
            pltpu.SemaphoreType.DMA((5,)),
            pltpu.SemaphoreType.DMA((5,)),
        ],
        compiler_params=WIDE,
        cost_estimate=pl.CostEstimate(
            flops=NORM_FLOPS, bytes_accessed=4 * n * rows * width, transcendentals=0
        ),
    )(order, gathered)


def main_kernel(order, normed_in, *refs):
    pieces = refs[0:16]
    grad_hidden, live = refs[16:18]
    gelu_out, turned, dx_out, row_out = refs[18:22]
    a_up, a_down, b_up, b_down = refs[22:26]
    normed, w, hidden, grad_in, dx, cols, sem_w, sem_n, sem_dx = refs[26:]
    n, width, tok = dx_out.shape
    rows = normed_in.shape[0]
    units = grad_hidden.shape[1]
    half = units // 2
    loads = [pltpu.make_async_copy(piece, w.at[k], sem_w.at[k]) for k, piece in enumerate(pieces)]
    quarter = SIDE * width
    loads_n = []
    for q in range(SIDE):
        part = (slice(None), pl.ds(q * quarter, quarter))
        loads_n.append(pltpu.make_async_copy(normed_in.at[part], normed.at[part], sem_n.at[q]))
    queue = [load for q in range(SIDE) for load in (loads_n[q], loads[2 * q], loads[2 * q + 1])] + loads[8:]
    for load in queue[:6]:
        load.start()
    later = queue[6:]

    def arrived(load):
        load.wait()
        if later:
            later.pop(0).start()

    def features(places, count):
        return jnp.concatenate([normed[0:count, p * width : (p + 1) * width] for p in places], axis=1)

    def weight_rows(s, q, j, count):
        return w[8 * s + 2 * q + j // 2, j % 2 * width : (j % 2 + count) * width, :]

    for s in range(2):
        total = None
        for q in range(SIDE):
            for j in (0, 2):
                if s == 0 and j == 0:
                    arrived(loads_n[q])
                arrived(loads[8 * s + 2 * q + j // 2])
                places = [q * SIDE + j + e if s == 0 else (j + e) * SIDE + q for e in (0, 1)]
                term = dot(features(places, rows), weight_rows(s, q, j, 2), 1, 0)
                total = term if total is None else total + term
        hidden[:, s * half : (s + 1) * half] = total

    def epilogue(r, carry):
        here = pl.ds(pl.multiple_of(r * STEP, STEP), STEP)
        h = hidden[here, :]
        cdf = 0.5 * (1.0 + lax.erf(h * INV_ROOT2))
        gelu_out[here, :] = (h * cdf).astype(BF16)
        slope = cdf + h * jnp.exp(-0.5 * h * h) * INV_ROOT_TWO_PI
        lives = jnp.concatenate([live[here, :]] * (units // 128), axis=1)
        g = (grad_hidden[here, :].astype(F32) * slope * lives).astype(BF16)
        grad_in[here, :] = g
        g = g.astype(F32)
        gained = g * hidden[tok : tok + 1, :]
        cols[0, here, :] = jnp.broadcast_to(jnp.sum(gained, axis=1, keepdims=True), (STEP, 128))
        cols[1, here, :] = jnp.broadcast_to(jnp.sum(g * h, axis=1, keepdims=True), (STEP, 128))
        return carry

    lax.fori_loop(0, tok // STEP, epilogue, 0)
    turned[...] = grad_in[...].T
    for k in range(2):
        row_out[k] = cols[k].T[0:8]

    saves = []
    for q in range(SIDE):
        for j in (0, 2):
            first = weight_rows(0, q, j, 2)
            second = jnp.concatenate([weight_rows(1, j + e, q, 1) for e in (0, 1)], axis=0)
            term = dot(jnp.concatenate([first, second], axis=1), turned[...], 1, 0).astype(BF16)
            for e in (0, 1):
                p = q * SIDE + j + e
                dx[p] = term[e * width : (e + 1) * width, :]
                saves.append(pltpu.make_async_copy(dx.at[p], dx_out.at[order[p]], sem_dx.at[p]))
                saves[-1].start()

    last = SIDE - 1
    for j, (a_out, b_out) in enumerate(((a_up, b_up), (a_down, b_down))):
        a = features([2 * j * SIDE + last, (2 * j + 1) * SIDE + last], tok)
        a_out[...] = dot(turned[0:half, :], a, 1, 0).astype(BF16)
        b = features([last * SIDE + 2 * j, last * SIDE + 2 * j + 1], tok)
        b_out[...] = dot(turned[half:, :], b, 1, 0).astype(BF16)
    for copy in saves:
        copy.wait()


def main(order, normed, wa, wb, grad_hidden, live):
    n, (rows, full) = order.shape[0], normed.shape
    tok, units = grad_hidden.shape
    shape = jax.ShapeDtypeStruct
    return pl.pallas_call(
        main_kernel,
        in_specs=[SMEM] + [HBM] * 17 + [VMEM, VMEM],
        out_specs=[VMEM, VMEM, HBM] + [VMEM] * 5,
        out_shape=[
            shape((tok, units), BF16),
            shape((units, tok), BF16),
            shape((n, full // n, tok), BF16),
            shape((2, 8, tok), F32),
        ]
        + [shape((units // 2, 2 * full // n), BF16)] * 4,
        scratch_shapes=[
            pltpu.VMEM((rows, full), BF16),
            pltpu.VMEM((n, 2 * full // n, units // 2), BF16),
            pltpu.VMEM((rows, units), F32),
            pltpu.VMEM((tok, units), BF16),
            pltpu.VMEM((n, full // n, tok), BF16),
            pltpu.VMEM((2, tok, 128), F32),
            pltpu.SemaphoreType.DMA((n,)),
            pltpu.SemaphoreType.DMA((SIDE,)),
            pltpu.SemaphoreType.DMA((n,)),
        ],
        compiler_params=FULL,
        cost_estimate=pl.CostEstimate(
            flops=4 * tok * units * full, bytes_accessed=40 * 2**20, transcendentals=0
        ),
    )(order, normed, *wa, *wb, grad_hidden, live)


def part_kernel(turned, c0, c1, c2, c3, b, *outs):
    n = len(outs) // 2
    half, size = outs[0].shape
    for k in range(n):
        a = jnp.concatenate([c[...] for c in (c0, c1, c2, c3)[k * SIDE // n : (k + 1) * SIDE // n]], axis=1)
        outs[k][...] = dot(turned[0:half, :], a, 1, 0).astype(BF16)
        right = b[:, k * size : (k + 1) * size]
        outs[n + k][...] = dot(turned[half:, :], right, 1, 0).astype(BF16)


def part(normed, turned, q, width):
    units, tok = turned.shape
    half = units // 2
    n = 1
    cut = [pl.BlockSpec((tok, width), lambda i, j=j: (0, j * SIDE + q)) for j in range(SIDE)]
    out = (half, SIDE // n * width)
    return pl.pallas_call(
        part_kernel,
        grid=(1,),
        in_specs=[pl.BlockSpec((units, tok), lambda i: (0, 0))]
        + cut
        + [pl.BlockSpec((tok, SIDE * width), lambda i: (0, q))],
        out_specs=[pl.BlockSpec(out, lambda i: (0, 0))] * (2 * n),
        out_shape=[jax.ShapeDtypeStruct(out, BF16)] * (2 * n),
        compiler_params=ROOM,
        cost_estimate=pl.CostEstimate(
            flops=2 * tok * units * SIDE * width, bytes_accessed=8 * 2**20, transcendentals=0
        ),
    )(turned, normed, normed, normed, normed, normed)


def along_x(s):
    return [(i, (i // SIDE + s) % SIDE * SIDE + i % SIDE) for i in range(SIDE * SIDE)]


def along_y(s):
    return [(i, i // SIDE * SIDE + (i % SIDE + s) % SIDE) for i in range(SIDE * SIDE)]


def move(x, path):
    return lax.ppermute(x, "dp", path)


def add(*xs):
    return sum(x.astype(F32) for x in xs)


def opposite_halves(ring, along):
    own, below, above = ring
    h = own.shape[0] // 2
    return [move(below[:h], along(1)), move(above[h:], along(-1))]


def join_kernel(*refs):
    at = 0
    for piece in refs[:-1]:
        refs[-1][at : at + piece.shape[0], :] = piece[...]
        at += piece.shape[0]


def join(pieces):
    rows, cols = sum(x.shape[0] for x in pieces), pieces[0].shape[1]
    return pl.pallas_call(
        join_kernel,
        in_specs=[VMEM] * len(pieces),
        out_specs=VMEM,
        out_shape=jax.ShapeDtypeStruct((rows, cols), BF16),
        compiler_params=ROOM,
        cost_estimate=pl.CostEstimate(flops=JOIN_FLOPS, bytes_accessed=4 * rows * cols, transcendentals=0),
    )(*pieces)


def spread(ring, low, along, other):
    high = join([ring[2]] + opposite_halves(ring, along))
    low = [low, move(low, other(1)), move(low, other(-1))]
    high = [high, move(high, other(1)), move(high, other(-1))]
    low.append(move(low[1], other(1)))
    high.append(move(high[2], other(-1)))
    return [x for pair in zip(low, high) for x in pair]


def ring_meet(minus, plus, up, down, along, axis):
    h = up.shape[axis]
    cut = lambda x, a, b: lax.slice_in_dim(x, a, b, axis=axis)
    up, down = move(up, along(1)), move(down, along(-1))
    plus = jnp.concatenate([add(cut(plus, 0, h), up).astype(BF16), cut(plus, h, 2 * h)], axis=axis)
    minus = jnp.concatenate([cut(minus, 0, h), add(cut(minus, h, 2 * h), down).astype(BF16)], axis=axis)
    return minus, plus


def on_device(
    patches, image_counts, image_seq, image_offset, segment_ids, norm_gain, w_up, grad_hidden
):
    tok, width = patches.shape
    n_dp, n_mp = lax.axis_size("dp"), lax.axis_size("mp")
    full = width * n_mp
    half = w_up.shape[1] // 2
    me = lax.axis_index("dp")
    ring = jnp.array(RING, jnp.int32) + SIDE
    order = ((me // SIDE + ring[None, :]) % SIDE * SIDE + (me % SIDE + ring[:, None]) % SIDE).reshape(-1)

    sent = pl.pallas_call(
        route_kernel,
        in_specs=[HBM] * 2,
        out_specs=VMEM,
        out_shape=jax.ShapeDtypeStruct((n_dp * SLOT, width), BF16),
        scratch_shapes=[
            pltpu.VMEM((n_dp * SLOT, tok), BF16),
            pltpu.SMEM((3, image_counts.shape[0]), jnp.int32),
            pltpu.VMEM(patches.shape, BF16),
            pltpu.SemaphoreType.DMA((2,)),
        ],
        compiler_params=WIDE,
    )(jnp.stack([image_counts, image_seq, image_offset]), patches)
    wa = [w_up[:, :half]]
    wb = [w_up[:, half:]]
    wa += [move(wa[0], along_x(1)), move(wa[0], along_x(-1))]
    wb += [move(wb[0], along_y(1)), move(wb[0], along_y(-1))]
    got = lax.all_to_all(sent, "dp", split_axis=0, concat_axis=0, tiled=True)
    mine = pl.pallas_call(
        place_kernel,
        in_specs=[VMEM, VMEM],
        out_specs=VMEM,
        out_shape=jax.ShapeDtypeStruct((tok + 16, width), BF16),
        scratch_shapes=[pltpu.VMEM((n_dp * SLOT, tok), BF16)],
        compiler_params=ROOM,
    )(got, norm_gain.reshape(1, width))
    gathered = lax.all_gather(mine, "mp", axis=0)
    live = jnp.broadcast_to((segment_ids.reshape(tok, 1) >= 0).astype(F32), (tok, 128))
    wa, wb, low_a, low_b, live = lax.optimization_barrier((wa, wb, join(wa[:2]), join(wb[:2]), live))
    wa = spread(wa, low_a, along_x, along_y)
    wb = spread(wb, low_b, along_y, along_x)

    normed, rows = norm(order, gathered, tok)
    row_mean, inverse_std = rows[0, 0:1], rows[1, 0:1]
    gelu_out, turned, terms, rows, *opposite = main(order, normed, wa, wb, grad_hidden, live)

    grad_normed = lax.psum_scatter(terms, "mp", scatter_dimension=0).astype(F32)

    plus, minus = part(normed, turned, 2, width), part(normed, turned, 1, width)
    a = ring_meet(minus[0], plus[0], *opposite[0:2], along_x, 1)
    b = ring_meet(minus[1], plus[1], *opposite[2:4], along_y, 1)
    a, b, normed, turned, rows = lax.optimization_barrier((a, b, normed, turned, rows))
    a = [move(a[0], along_x(-1)), move(a[1], along_x(1))]
    b = [move(b[0], along_y(-1)), move(b[1], along_y(1))]
    own = part(normed, turned, 0, width)
    a, b = add(own[0], *a), add(own[1], *b)

    def finish(x, along):
        cut = [x[:, q * width : (q + 1) * width] for q in range(SIDE)]
        sent = [c.astype(BF16) for c in cut[1:]]
        h = half // 2
        minus, plus = ring_meet(sent[0], sent[1], sent[2][:h], sent[2][h:], along, 0)
        return add(cut[0], move(minus, along(-1)), move(plus, along(1)))

    grad_scale = 1.0 / math.sqrt(tok * n_dp)
    grad_w = (jnp.concatenate([finish(a, along_y), finish(b, along_x)], axis=0) * grad_scale).T

    sums = lax.all_to_all(
        jnp.broadcast_to(rows[:, 0].reshape(1, 2 * tok), (n_mp, 2 * tok)),
        "mp",
        split_axis=0,
        concat_axis=0,
        tiled=True,
    )
    sums = jnp.sum(sums, axis=0, keepdims=True) / full
    first_mean, second_mean = sums[:, :tok], sums[:, tok:]

    scaled = (mine[:tok].T.astype(F32) - row_mean) * inverse_std
    grad_scaled = grad_normed * norm_gain.astype(F32)[:, None]
    grad_packed = inverse_std * (grad_scaled - first_mean - scaled * second_mean)
    gain_part = jnp.sum(grad_normed * scaled, axis=1)[None, :]
    gain_part = lax.all_to_all(
        jnp.broadcast_to(gain_part, (n_dp, width)), "dp", split_axis=0, concat_axis=0, tiled=True
    )
    grad_gain = jnp.sum(gain_part, axis=0) * grad_scale
    return (gelu_out, grad_w, grad_gain, grad_packed.astype(BF16).T)


def solution(mesh):
    return jax.shard_map(
        on_device,
        mesh=mesh,
        in_specs=(
            P("dp", "mp"),
            P("dp"),
            P("dp"),
            P("dp"),
            P("dp", None),
            P("mp"),
            P("dp", "mp"),
            P("dp", "mp"),
        ),
        out_specs=(P("dp", "mp"), P("dp", "mp"), P("mp"), P("dp", "mp")),
        check_vma=False,
    )
```
